128 devices in a mesh: frame: 16 (over x, y), tile: 8 (over z, core).
Axes of the slice: x: 4, y: 4, z: 4, core: 2. Of those that a mesh axis runs over, the one named last changes fastest.
Arguments:
- grid: bfloat16 [64, 32, 32, 2048], P(None, 'frame', None, 'tile'), may hold values from -6 to 6
- conv_weight: bfloat16 [9, 64, 8], replicated, may hold values from -0.75 to 0.75
- conv_bias: float32 [64], replicated, may hold values from -3 to 3
- depth_kernel: float32 [4, 3, 64], replicated, may hold values from -3 to 3
- point_weight: bfloat16 [4, 64, 64], replicated, may hold values from -0.75 to 0.75
- occupied: int32 [8, 32], P('tile'), may hold values from 0 to 63, as said below
- counts: int32 [8], P('tile'), may hold values from 10 to 32, as said below
Outputs:
- features: bfloat16 [64, 32, 32, 2048], P(None, 'frame', None, 'tile')
The draws below stay inside these ranges and needn't reach their ends.
Inputs may be any that keep to these rules, and one draw needn't show every extreme that they name: Each row holds 32 distinct block numbers of its tile; its first counts[t] entries are the occupied blocks, the rest are unoccupied blocks used as padding. `counts`: some tile's list is fully occupied, and some tile has exactly the fewest occupied entries.
All inputs are finite; a program needn't handle non-finite values.
Results may differ from the reference program's by a relative error of at most 0.0051.
Values may be sent and summed in bfloat16 or wider, within the bound.
A program may use at most 128 MiB of HBM per device.

```python
import jax
import jax.numpy as jnp
from jax import lax

C = 64
GROUP = 8
LAYERS = 4
ROWS = 32
WDEV = 256
FRAMES = 32
WIDTH = 2048
K_SLOTS = 32
N_TILE = 8


def swapped(values, first, second):
    positions = jnp.arange(values.shape[0], dtype=jnp.int32)
    first_value = values[first]
    second_value = values[second]
    return jnp.where(positions == first, second_value, jnp.where(positions == second, first_value, values))


def one_permutation(subkey):
    return jax.random.permutation(subkey, ROWS * WDEV // 128)


def draw_occupied(key, part):
    key = jax.random.fold_in(key, 11)
    blocks_total = ROWS * WDEV // 128
    subkeys = jax.random.split(key, N_TILE + 1)
    orders = jax.vmap(one_permutation)(subkeys[:N_TILE]).astype(jnp.int32)
    chosen_tile = jax.random.randint(subkeys[N_TILE], (), 0, N_TILE)
    picked_row = orders[chosen_tile]
    high_at = jnp.argmax(picked_row == blocks_total - 1).astype(jnp.int32)
    picked_row = swapped(picked_row, 0, high_at)
    low_at = jnp.argmax(picked_row == 0).astype(jnp.int32)
    picked_row = swapped(picked_row, 1, low_at)
    orders = orders.at[chosen_tile].set(picked_row)
    return orders[:, :K_SLOTS].astype(jnp.int32)


def draw_counts(key, part):
    key = jax.random.fold_in(key, 23)
    first_key, second_key = jax.random.split(key)
    drawn = jax.random.randint(first_key, (N_TILE,), K_SLOTS // 3, K_SLOTS + 1)
    full_tile = jax.random.randint(second_key, (), 0, N_TILE)
    short_tile = (full_tile + 1) % N_TILE
    positions = jnp.arange(N_TILE, dtype=jnp.int32)
    drawn = jnp.where(positions == short_tile, K_SLOTS // 3, drawn)
    return jnp.where(positions == full_tile, K_SLOTS, drawn).astype(jnp.int32)


def steps_of(key, extent, shards, low, high):
    factor_of, own = 1.0, jax.random.fold_in(key, 6)
    for dim, parts in shards:
        heights = jnp.exp(jax.random.uniform(jax.random.fold_in(own, dim), (parts,), jnp.float32, low / len(shards), high / len(shards)))
        factor_of = factor_of * jnp.repeat(heights, extent[dim] // parts).reshape([-1 if axis == dim else 1 for axis in range(len(extent))])
    return factor_of


def centred(own_key, extent, scale, limit, pieces=(), kind=jnp.bfloat16):
    values = scale * jax.random.normal(own_key, extent, jnp.float32)
    if pieces:
        values = values * steps_of(own_key, extent, pieces, -0.22, 0.18)
    return jnp.clip(values, -limit, limit).astype(kind)


def setup_inputs(seed: int = 0) -> dict:
    key_list = jax.random.split(jax.random.key(seed), 8)
    grid = centred(key_list[0], (C, FRAMES, ROWS, WIDTH), 1.0, 6.0, ((1, 16), (3, 8)))
    conv_weight = centred(key_list[1], (9, C, GROUP), (9 * GROUP) ** -0.5, 0.75)
    conv_bias = centred(key_list[2], (C,), 0.5, 3.0, (), jnp.float32)
    depth_kernel = centred(key_list[3], (LAYERS, 3, C), 0.5, 3.0, (), jnp.float32)
    point_weight = centred(key_list[4], (LAYERS, C, C), C ** -0.5, 0.75)
    occupied = draw_occupied(jax.random.fold_in(key_list[7], 71), 0)
    counts = draw_counts(jax.random.fold_in(key_list[7], 71), 0)
    return {"grid": grid, "conv_weight": conv_weight, "conv_bias": conv_bias, "depth_kernel": depth_kernel, "point_weight": point_weight, "occupied": occupied, "counts": counts}


def shifted(series, amount):
    if amount == 0:
        return series
    frames = series.shape[1]
    if amount >= frames:
        return jnp.zeros_like(series)
    leading = jnp.zeros_like(series[:, :amount])
    return jnp.concatenate([leading, series[:, :frames - amount]], axis=1)


def temporal(blocks, depth_kernel, point_weight):
    current = blocks.astype(jnp.float32)
    for layer_idx in range(depth_kernel.shape[0]):
        spacing = 2 ** layer_idx
        blended = jnp.zeros_like(current)
        for offset in range(depth_kernel.shape[1]):
            blended = blended + depth_kernel[layer_idx, offset][:, None, None, None] * shifted(current, offset * spacing)
        squashed = jax.nn.silu(blended).astype(jnp.bfloat16)
        current = current + jnp.einsum("oc,cfsn->ofsn", point_weight[layer_idx].astype(jnp.float32), squashed.astype(jnp.float32))
    return current.astype(jnp.bfloat16)


def spatial(padded, center, conv_weight, conv_bias):
    channels, frames, height, columns = center.shape
    group_count = channels // GROUP
    grouped = padded.reshape(group_count, GROUP, frames, height + 2, columns + 2).astype(jnp.float32)
    summed = jnp.zeros((group_count, GROUP, frames, height, columns), jnp.float32)
    for tap_row in range(3):
        for tap_col in range(3):
            window = grouped[:, :, :, tap_row:tap_row + height, tap_col:tap_col + columns]
            kernel = conv_weight[tap_row * 3 + tap_col].reshape(group_count, GROUP, GROUP).astype(jnp.float32)
            summed = summed + jnp.einsum("goi,gifrw->gofrw", kernel, window)
    activation = summed.reshape(channels, frames, height, columns) + conv_bias[:, None, None, None]
    return (center.astype(jnp.float32) + jax.nn.silu(activation)).astype(jnp.bfloat16)


def reference(grid, conv_weight, conv_bias, depth_kernel, point_weight, occupied, counts):
    channels, frames, height, width = grid.shape
    tile_width = width // N_TILE
    padded = jnp.pad(grid, ((0, 0), (0, 0), (1, 1), (1, 1)))

    def per_tile(tile_idx):
        tile_idx = tile_idx.astype(jnp.int32)
        strip_part = lax.dynamic_slice_in_dim(padded, tile_idx * tile_width, tile_width + 2, 3)
        center = strip_part[:, :, 1:-1, 1:-1]
        hidden = spatial(strip_part, center, conv_weight, conv_bias)
        blocks = hidden.reshape(channels, frames, height * (tile_width // 128), 128)
        block_ids = occupied[tile_idx]
        picked = jnp.take(blocks, block_ids, axis=2)
        updated = temporal(picked, depth_kernel, point_weight)
        live_slots = jnp.arange(block_ids.shape[0], dtype=jnp.int32) < counts[tile_idx]
        chosen = jnp.where(live_slots[None, None, :, None], updated, picked)
        blocks = blocks.at[:, :, block_ids].set(chosen)
        return blocks.reshape(channels, frames, height, tile_width)

    results = lax.map(per_tile, jnp.arange(N_TILE, dtype=jnp.int32))
    return results.transpose(1, 2, 3, 0, 4).reshape(channels, frames, height, width)
```

```python
import functools

import jax
import jax.numpy as jnp
from jax import lax
from jax.experimental import pallas as pl
from jax.experimental.pallas import tpu as pltpu
from jax.sharding import PartitionSpec as P

MESH = pl.DeviceIdType.MESH
F32 = jnp.float32
BF16 = jnp.bfloat16

HOPS = (
    (2, 2), (2, 1), (2, 3), (1, 2), (3, 2), (2, 0), (0, 2),
    (1, 1), (3, 3), (1, 3), (3, 1), (1, 0), (3, 0), (0, 1), (0, 3),
)


def rows(shape):
    return lax.broadcasted_iota(jnp.int32, shape, 0)


def cols(shape):
    return lax.broadcasted_iota(jnp.int32, shape, 1)


def one_hot(mask):
    return jnp.where(mask, 1.0, 0.0).astype(BF16)


def dot(lhs, rhs, contract=((1,), (0,))):
    return lax.dot_general(lhs, rhs, (contract, ((), ())), preferred_element_type=F32)


def gated(half):
    return half + half * jnp.tanh(half)


def kernel(
    grid_hbm, weight_ref, bias_ref, depth_ref, point_ref, occupied_ref, count_ref,
    out_ref,
    cells, wide, lanes, band, slot_band, pick, place, covered, mix, taps, bias_col, half_col,
    edge_out, edge_in, hidden, outgoing, incoming, state, answer, returned,
    load_sem, edge_send, edge_recv, send_sems, recv_sems,
):
    me = lax.axis_index("frame")
    tile = lax.axis_index("tile")
    row, col = me // 4, me % 4
    right, left = {"tile": (tile + 1) % 8}, {"tile": (tile + 7) % 8}

    def peer(hop):
        return ((row + hop[0]) % 4) * 4 + (col + hop[1]) % 4

    barrier = pltpu.get_barrier_semaphore()
    for neighbour in (right, left):
        pl.semaphore_signal(barrier, inc=1, device_id=neighbour, device_id_type=MESH)
    for hop in HOPS:
        pl.semaphore_signal(barrier, inc=1, device_id={"frame": peer(hop)}, device_id_type=MESH)
    load = pltpu.make_async_copy(grid_hbm, cells, load_sem)
    load.start()

    spread = one_hot((cols((8, 256)) >> 5) == rows((8, 256)))
    for tap in range(9):
        lanes[tap] = 0.5 * dot(weight_ref[tap], spread, ((0,), (0,)))
    delta = (cols((32, 256)) & 31) - rows((32, 256))

    @pl.loop(0, 8)
    def _(g):
        for dc in range(3):
            for o in range(8):
                value = jnp.zeros((32, 256), F32)
                for dr in range(3):
                    line = lanes[3 * dr + dc, pl.ds(8 * g + o, 1), :]
                    value = jnp.where(delta == dr - 1, line, value)
                band[g, o * 32 : (o + 1) * 32, dc * 256 : (dc + 1) * 256] = value.astype(BF16)

    listed = occupied_ref[...]
    row_of = (listed >> 1).astype(F32)
    half_of = (listed & 1).astype(F32)
    own = cols((256, 32)) == (rows((256, 32)) >> 3)
    row_col = jnp.sum(jnp.where(own, row_of, 0.0), axis=1, keepdims=True)
    half_col[...] = jnp.broadcast_to(jnp.sum(jnp.where(own, half_of, 0.0), axis=1, keepdims=True), (256, 128))
    r2, c2 = rows((256, 256)), cols((256, 256))
    pick[...] = one_hot(((r2 & 7) == (c2 >> 5)) & ((c2 & 31).astype(F32) == row_col))
    expand = one_hot((cols((32, 256)) >> 3) == rows((32, 256)))
    row_lane = dot(jnp.broadcast_to(row_of, (8, 32)).astype(BF16), expand)[0:1]
    half_lane = dot(jnp.broadcast_to(half_of, (8, 32)).astype(BF16), expand)[0:1]
    live = (c2 >> 3) < count_ref[0]
    target = ((r2 >> 5) == (c2 & 7)) & ((r2 & 31).astype(F32) == row_lane) & live
    for h in range(2):
        chosen = jnp.where(target & (half_lane == float(h)), 1.0, 0.0)
        place[h * 256 : (h + 1) * 256, :] = chosen.astype(BF16)
        covered[:, h * 128 : (h + 1) * 128] = jnp.broadcast_to(jnp.sum(chosen, axis=1, keepdims=True), (256, 128))

    @pl.loop(0, 8)
    def _(g):
        slot_band[g] = dot(pick[...], band[g]).astype(BF16)

    diagonal = rows((64, 64)) == cols((64, 64))
    bias_half = jnp.sum(jnp.where(diagonal, 0.5 * bias_ref[...], 0.0), axis=1, keepdims=True)
    bias_col[...] = jnp.broadcast_to(bias_half, (64, 256))
    for layer in range(4):
        for j in range(3):
            line = 0.5 * depth_ref[j, layer : layer + 1, :]
            column = jnp.sum(jnp.where(diagonal, line, 0.0), axis=1, keepdims=True)
            taps[3 * layer + j] = jnp.broadcast_to(column, (64, 128))
    repeat = one_hot((rows((256, 64)) & 63) == cols((256, 64)))
    for layer in range(4):
        tall = dot(repeat, point_ref[layer]).astype(BF16)
        full = dot(tall, repeat, ((1,), (1,)))
        mix[layer] = jnp.where((r2 >> 6) == (c2 >> 6), full, 0.0).astype(BF16)

    load.wait()
    r3, c3 = rows((32, 256)), cols((32, 256))

    def edges(n, total):
        block = cells[pl.ds(8 * (n // 2), 8), n % 2].reshape(256, 256)
        wanted = ((r3 == n) & (c3 == 255)) | ((r3 == 16 + n) & (c3 == 0))
        return total + dot(one_hot(wanted), block, ((1,), (1,)))

    both = lax.fori_loop(0, 16, edges, jnp.zeros((32, 256), F32)).astype(BF16)
    edge_out[0] = both[:16]
    edge_out[1] = both[16:]
    pl.semaphore_wait(barrier, 17)
    edge_copies = []
    for side, neighbour in enumerate((right, left)):
        copy = pltpu.make_async_remote_copy(
            src_ref=edge_out.at[side],
            dst_ref=edge_in.at[side],
            send_sem=edge_send.at[side],
            recv_sem=edge_recv.at[side],
            device_id=neighbour,
            device_id_type=MESH,
        )
        copy.start()
        edge_copies.append(copy)

    lane = cols((256, 256))

    @pl.loop(0, 16)
    def _(n):
        block = cells[pl.ds(8 * (n // 2), 8), n % 2].reshape(256, 256)
        wide[n, 256:512] = block
        block = block.astype(F32)
        wide[n, 0:256] = jnp.where(lane == 0, 0.0, pltpu.roll(block, 1, 1)).astype(BF16)
        wide[n, 512:768] = jnp.where(lane == 255, 0.0, pltpu.roll(block, 255, 1)).astype(BF16)

    for copy in edge_copies:
        copy.wait()
    arrived = edge_in[...].reshape(32, 256).astype(F32)
    there = ((r3 < 16) & (tile > 0)) | ((r3 >= 16) & (tile < 7))
    halo = jnp.where(there, arrived, 0.0).T.astype(BF16)

    @pl.loop(0, 16)
    def _(n):
        put = one_hot(((r3 == n) & (c3 == 0)) | ((r3 == 16 + n) & (c3 == 255)))
        fix = dot(halo, put).astype(BF16)
        wide[n, 0:256, 0:128] += fix[:, :128]
        wide[n, 512:768, 128:256] += fix[:, 128:]

    def slots(s):
        lo = 128 * s

        @pl.loop(0, 4)
        def _(pair):
            second = half_col[lo : lo + 128] > 0.5
            for f in range(2):
                parts = []
                for e in range(2):
                    g = 2 * pair + e
                    act = dot(slot_band[g, lo : lo + 128, :], wide[2 * g + f])
                    plain = dot(pick[lo : lo + 128, :], wide[2 * g + f, 256:512])
                    act = jnp.where(second, act[:, 128:], act[:, :128]).reshape(16, 8, 128)
                    plain = jnp.where(second, plain[:, 128:], plain[:, :128]).reshape(16, 8, 128)
                    act = act + bias_col[pl.ds(8 * g, 8), 0:128]
                    parts.append(plain + gated(act))
                joined = jnp.concatenate(parts, axis=1).astype(BF16)
                outgoing[16 * s : 16 * s + 16, f, pl.ds(16 * pair, 16), :] = joined

    copies = []

    def send(stage, source, target):
        for hop in HOPS:
            to = peer(hop)
            copy = pltpu.make_async_remote_copy(
                src_ref=source(to),
                dst_ref=target,
                send_sem=send_sems.at[stage],
                recv_sem=recv_sems.at[stage],
                device_id={"frame": to},
                device_id_type=MESH,
            )
            copy.start()

    def whole(stage, ref):
        return pltpu.make_async_remote_copy(
            src_ref=ref,
            dst_ref=ref,
            send_sem=send_sems.at[stage],
            recv_sem=recv_sems.at[stage],
            device_id={"frame": peer(HOPS[0])},
            device_id_type=MESH,
        )

    for s in range(2):
        slots(s)
        send(s, lambda to, s=s: outgoing.at[16 * s + to], incoming.at[s, me])
        incoming[s, me] = outgoing[16 * s + me]

    @pl.loop(0, 8)
    def _(g):
        for f in range(2):
            act = dot(band[g], wide[2 * g + f])
            for o in range(8):
                half = act[o * 32 : (o + 1) * 32] + bias_col[pl.ds(8 * g + o, 1), :]
                value = cells[8 * g + o, f].astype(F32) + gated(half)
                hidden[8 * g + o, f] = value.astype(BF16)

    def temporal(s):
        state[0:16] = jnp.zeros((16, 64, 128), F32)

        @pl.loop(0, 16)
        def _(p):
            state[pl.ds(16 + 2 * p, 2)] = incoming[s, p].astype(F32)

        for layer in range(4):
            d = 2**layer

            @pl.loop(0, 4)
            def _(i):
                base = 40 - 8 * i
                now = state[pl.ds(base, 8)]
                half = taps[3 * layer] * now
                half = half + taps[3 * layer + 1] * state[pl.ds(base - d, 8)]
                half = half + taps[3 * layer + 2] * state[pl.ds(base - 2 * d, 8)]
                squashed = gated(half).astype(BF16)
                pair = [squashed[0:4].reshape(256, 128), squashed[4:8].reshape(256, 128)]
                mixed = dot(mix[layer], jnp.concatenate(pair, axis=1))
                for h in range(2):
                    new = now[4 * h : 4 * h + 4] + mixed[:, 128 * h : 128 * h + 128].reshape(4, 64, 128)
                    if layer < 3:
                        state[pl.ds(base + 4 * h, 4)] = new
                    else:
                        answer[s, pl.ds(12 - 4 * i + 2 * h, 2)] = new.reshape(2, 2, 64, 128).astype(BF16)

    for s in range(2):
        whole(s, incoming.at[s, pl.ds(0, 15)]).wait_recv()
        temporal(s)
        send(2 + s, lambda to, s=s: answer.at[s, to], returned.at[16 * s + me])
        returned[16 * s + me] = answer[s, me]

    for s in range(2):
        whole(2 + s, returned.at[pl.ds(0, 15)]).wait_recv()

    @pl.loop(0, 4)
    def _(pair):
        split = [returned[:, f, pl.ds(16 * pair, 16), :].astype(F32) for f in range(2)]
        for e in range(2):
            g = 2 * pair + e
            both = [part[:, 8 * e : 8 * e + 8].reshape(256, 128) for part in split]
            value = dot(place[...], jnp.concatenate(both, axis=1).astype(BF16))
            for f in range(2):
                for h in range(2):
                    span = slice(128 * h, 128 * h + 128)
                    new = value[256 * h : 256 * h + 256, 128 * f : 128 * f + 128]
                    old = hidden[pl.ds(8 * g, 8), f, :, span].reshape(256, 128).astype(F32)
                    new = jnp.where(covered[:, span] > 0.5, new, old)
                    out_ref[pl.ds(8 * g, 8), f, :, span] = new.reshape(8, 32, 128).astype(BF16)

    for s in range(2):
        whole(s, outgoing.at[pl.ds(0, 15)]).wait_send()
        whole(2 + s, answer.at[s, pl.ds(0, 15)]).wait_send()


def on_device(grid, conv_weight, conv_bias, depth_kernel, point_weight, occupied, counts):
    vmem = pl.BlockSpec(memory_space=pltpu.VMEM)
    buffers = [
        ((64, 2, 32, 256), BF16),
        ((16, 768, 256), BF16),
        ((9, 64, 256), F32),
        ((8, 256, 768), BF16),
        ((8, 256, 768), BF16),
        ((256, 256), BF16),
        ((512, 256), BF16),
        ((256, 256), F32),
        ((4, 256, 256), BF16),
        ((12, 64, 128), F32),
        ((64, 256), F32),
        ((256, 128), F32),
        ((2, 16, 256), BF16),
        ((2, 16, 256), BF16),
        ((64, 2, 32, 256), BF16),
        ((32, 2, 64, 128), BF16),
        ((2, 16, 2, 64, 128), BF16),
        ((48, 64, 128), F32),
        ((2, 16, 2, 64, 128), BF16),
        ((32, 2, 64, 128), BF16),
    ]
    return pl.pallas_call(
        kernel,
        out_shape=jax.ShapeDtypeStruct(grid.shape, grid.dtype),
        in_specs=[pl.BlockSpec(memory_space=pl.ANY)] + [vmem] * 5 + [pl.BlockSpec(memory_space=pltpu.SMEM)],
        out_specs=vmem,
        scratch_shapes=[pltpu.VMEM(shape, kind) for shape, kind in buffers]
        + [
            pltpu.SemaphoreType.DMA,
            pltpu.SemaphoreType.DMA((2,)),
            pltpu.SemaphoreType.DMA((2,)),
            pltpu.SemaphoreType.DMA((4,)),
            pltpu.SemaphoreType.DMA((4,)),
        ],
        compiler_params=pltpu.CompilerParams(
            collective_id=0, has_side_effects=True, vmem_limit_bytes=56 * 1024 * 1024
        ),
        cost_estimate=pl.CostEstimate(flops=4_000_000_000, bytes_accessed=4 << 20, transcendentals=3 << 20),
    )(
        grid,
        conv_weight.transpose(0, 2, 1),
        conv_bias.reshape(1, 64),
        depth_kernel.transpose(1, 0, 2),
        point_weight,
        occupied,
        counts,
    )


def solution(mesh):
    placed = (P(None, "frame", None, "tile"), P(), P(), P(), P(), P("tile", None), P("tile"))
    return jax.shard_map(
        on_device,
        mesh=mesh,
        in_specs=placed,
        out_specs=P(None, "frame", None, "tile"),
        check_vma=False,
    )
```

```python
import functools

import jax
import jax.numpy as jnp
from jax import lax
from jax.experimental import pallas as pl
from jax.experimental.pallas import tpu as pltpu
from jax.sharding import PartitionSpec as P

MESH = pl.DeviceIdType.MESH
F32 = jnp.float32
BF16 = jnp.bfloat16
UNROLL = 4

HOPS = (
    (2, 2), (2, 1), (2, 3), (1, 2), (3, 2), (2, 0), (0, 2),
    (1, 1), (3, 3), (1, 3), (3, 1), (1, 0), (3, 0), (0, 1), (0, 3),
)


def rows(shape):
    return lax.broadcasted_iota(jnp.int32, shape, 0)


def cols(shape):
    return lax.broadcasted_iota(jnp.int32, shape, 1)


def one_hot(mask):
    return jnp.where(mask, 1.0, 0.0).astype(BF16)


def dot(lhs, rhs, contract=((1,), (0,))):
    return lax.dot_general(lhs, rhs, (contract, ((), ())), preferred_element_type=F32)


def gated(half):
    return half + half * jnp.tanh(half)


def kernel(
    grid_hbm, weight_hbm, bias_hbm, depth_hbm, point_hbm, occupied_hbm, count_hbm,
    out_ref,
    weight_ref, bias_ref, depth_ref, point_ref, occupied_ref, count_ref, cells, wide, lanes, band,
    slot_band, pick, place, covered, mix, taps, bias_col, row_col, half_col,
    edge_out, edge_in, hidden, outgoing, incoming, state, answer, returned,
    load_sems, edge_send, edge_recv, send_sems, recv_sems,
):
    me = lax.axis_index("frame")
    tile = lax.axis_index("tile")
    row, col = me // 4, me % 4
    right, left = {"tile": (tile + 1) % 8}, {"tile": (tile + 7) % 8}

    def peer(hop):
        return ((row + hop[0]) % 4) * 4 + (col + hop[1]) % 4

    barrier = pltpu.get_barrier_semaphore()
    for neighbour in (right, left):
        pl.semaphore_signal(barrier, inc=1, device_id=neighbour, device_id_type=MESH)
    for hop in HOPS:
        pl.semaphore_signal(barrier, inc=1, device_id={"frame": peer(hop)}, device_id_type=MESH)
    sources = (grid_hbm, weight_hbm, bias_hbm, depth_hbm, point_hbm, occupied_hbm, count_hbm)
    targets = (cells, weight_ref, bias_ref, depth_ref, point_ref, occupied_ref, count_ref)
    loads = []
    for i, (source, target) in enumerate(zip(sources, targets)):
        loads.append(pltpu.make_async_copy(source, target, load_sems.at[i]))
        loads[i].start()

    loads[0].wait()
    lane, lane_wide = cols((256, 128)), cols((256, 256))
    nought = jnp.zeros((256, 256), BF16)

    def shift(n, edge):
        block = cells[pl.ds(8 * (n // 2), 8), n % 2].reshape(256, 256)
        wide[n, 256:512] = block
        wide[n, 0:256] = jnp.where(lane_wide == 0, nought, pltpu.roll(block, 1, 1))
        wide[n, 512:768] = jnp.where(lane_wide == 255, nought, pltpu.roll(block, 255, 1))
        edge = jnp.where(lane == n, pltpu.roll(block[:, 128:], n + 1, 1), edge)
        return jnp.where(lane == 16 + n, pltpu.roll(block[:, :128], 16 + n, 1), edge)

    edge_out[...] = lax.fori_loop(0, 16, shift, nought[:, :128], unroll=UNROLL)

    for load in loads[1:]:
        load.wait()
    r2, c2 = rows((256, 256)), cols((256, 256))
    listed = occupied_ref[...]
    row_of = (listed >> 1).astype(F32)
    half_of = (listed & 1).astype(F32)
    own = cols((256, 32)) == (rows((256, 32)) >> 3)
    row_here = jnp.sum(jnp.where(own, row_of, 0.0), axis=1, keepdims=True)
    row_col[...] = jnp.broadcast_to(row_here, (256, 256))
    half_col[...] = jnp.broadcast_to(jnp.sum(jnp.where(own, half_of, 0.0), axis=1, keepdims=True), (256, 128))
    pick[...] = one_hot(((r2 & 7) == (c2 >> 5)) & ((c2 & 31).astype(F32) == row_here))
    diagonal = rows((64, 64)) == cols((64, 64))
    bias_half = jnp.sum(jnp.where(diagonal, 0.5 * bias_ref[...], 0.0), axis=1, keepdims=True)
    bias_col[...] = jnp.broadcast_to(bias_half, (64, 256))

    spread = one_hot((cols((8, 256)) >> 5) == rows((8, 256)))
    for tap in range(9):
        lanes[tap] = 0.5 * dot(weight_ref[tap], spread, ((0,), (0,)))
    row_lanes = (cols((8, 256)) & 31).astype(F32)

    @pl.loop(0, 16)
    def _(pair):
        start = pl.multiple_of(16 * pair, 16)
        delta = [row_lanes - row_col[pl.ds(start + 8 * k, 8)] for k in range(2)]
        for g in range(8):
            for dc in range(3):
                parts = []
                for k in range(2):
                    value = jnp.zeros((8, 256), F32)
                    for dr in range(3):
                        value = jnp.where(delta[k] == dr - 1.0, lanes[3 * dr + dc, 8 * g : 8 * g + 8], value)
                    parts.append(value)
                both = jnp.concatenate(parts, axis=0).astype(BF16)
                slot_band[g, pl.ds(start, 16), dc * 256 : (dc + 1) * 256] = both

    pl.semaphore_wait(barrier, 17)
    edge_copies = []
    for side, neighbour in enumerate((right, left)):
        copy = pltpu.make_async_remote_copy(
            src_ref=edge_out,
            dst_ref=edge_in.at[side],
            send_sem=edge_send.at[side],
            recv_sem=edge_recv.at[side],
            device_id=neighbour,
            device_id_type=MESH,
        )
        copy.start()
        edge_copies.append(copy)

    offset = (cols((32, 256)) & 31) - rows((32, 256))

    @pl.loop(0, 8)
    def _(g):
        for dc in range(3):
            for o in range(8):
                value = jnp.zeros((32, 256), F32)
                for dr in range(3):
                    line = lanes[3 * dr + dc, pl.ds(8 * g + o, 1), :]
                    value = jnp.where(offset == dr - 1, line, value)
                band[g, o * 32 : (o + 1) * 32, dc * 256 : (dc + 1) * 256] = value.astype(BF16)

    expand = one_hot((cols((32, 256)) >> 3) == rows((32, 256)))
    row_lane = dot(jnp.broadcast_to(row_of, (8, 32)).astype(BF16), expand)[0:1]
    half_lane = dot(jnp.broadcast_to(half_of, (8, 32)).astype(BF16), expand)[0:1]
    live = (c2 >> 3) < count_ref[0]
    target = ((r2 >> 5) == (c2 & 7)) & ((r2 & 31).astype(F32) == row_lane) & live
    for h in range(2):
        chosen = jnp.where(target & (half_lane == float(h)), 1.0, 0.0)
        place[h * 256 : (h + 1) * 256, :] = chosen.astype(BF16)
        covered[:, h * 128 : (h + 1) * 128] = jnp.broadcast_to(jnp.sum(chosen, axis=1, keepdims=True), (256, 128))

    for layer in range(4):
        for j in range(3):
            line = 0.5 * depth_ref[j, layer : layer + 1, :]
            column = jnp.sum(jnp.where(diagonal, line, 0.0), axis=1, keepdims=True)
            taps[3 * layer + j] = jnp.broadcast_to(column, (64, 128))
    repeat = one_hot((rows((256, 64)) & 63) == cols((256, 64)))
    for layer in range(4):
        tall = dot(repeat, point_ref[layer]).astype(BF16)
        full = dot(tall, repeat, ((1,), (1,)))
        mix[layer] = jnp.where((r2 >> 6) == (c2 >> 6), full, 0.0).astype(BF16)

    for copy in edge_copies:
        copy.wait()
    from_left = jnp.where(tile > 0, edge_in[0], nought[:, :128])
    from_right = jnp.where(tile < 7, edge_in[1], nought[:, :128])

    def fix(n, carry):
        old = wide[n, 0:256, 0:128]
        wide[n, 0:256, 0:128] = jnp.where(lane == 0, pltpu.roll(from_left, (128 - n) % 128, 1), old)
        old = wide[n, 512:768, 128:256]
        wide[n, 512:768, 128:256] = jnp.where(lane == 127, pltpu.roll(from_right, 111 - n, 1), old)
        return carry

    lax.fori_loop(0, 16, fix, 0, unroll=UNROLL)

    def slots(s):
        lo = 128 * s

        @pl.loop(0, 4, unroll=2)
        def _(pair):
            second = half_col[lo : lo + 128] > 0.5
            for f in range(2):
                parts = []
                for e in range(2):
                    g = 2 * pair + e
                    act = dot(slot_band[g, lo : lo + 128, :], wide[2 * g + f])
                    plain = dot(pick[lo : lo + 128, :], wide[2 * g + f, 256:512])
                    act = jnp.where(second, act[:, 128:], act[:, :128]).reshape(16, 8, 128)
                    plain = jnp.where(second, plain[:, 128:], plain[:, :128]).reshape(16, 8, 128)
                    act = act + bias_col[pl.ds(8 * g, 8), 0:128]
                    parts.append(plain + gated(act))
                joined = jnp.concatenate(parts, axis=1).astype(BF16)
                outgoing[16 * s : 16 * s + 16, f, pl.ds(16 * pair, 16), :] = joined

    copies = []

    def send(stage, source, target):
        for hop in HOPS:
            to = peer(hop)
            copy = pltpu.make_async_remote_copy(
                src_ref=source(to),
                dst_ref=target,
                send_sem=send_sems.at[stage],
                recv_sem=recv_sems.at[stage],
                device_id={"frame": to},
                device_id_type=MESH,
            )
            copy.start()

    def whole(stage, ref):
        return pltpu.make_async_remote_copy(
            src_ref=ref,
            dst_ref=ref,
            send_sem=send_sems.at[stage],
            recv_sem=recv_sems.at[stage],
            device_id={"frame": peer(HOPS[0])},
            device_id_type=MESH,
        )

    for s in range(2):
        slots(s)
        send(s, lambda to, s=s: outgoing.at[16 * s + to], incoming.at[s, me])
        incoming[s, me] = outgoing[16 * s + me]

    @pl.loop(0, 8, unroll=2)
    def _(g):
        for f in range(2):
            act = dot(band[g], wide[2 * g + f])
            for o in range(8):
                half = act[o * 32 : (o + 1) * 32] + bias_col[pl.ds(8 * g + o, 1), :]
                value = cells[8 * g + o, f].astype(F32) + gated(half)
                hidden[8 * g + o, f] = value.astype(BF16)

    def temporal(s):
        state[0:16] = jnp.zeros((16, 64, 128), F32)

        @pl.loop(0, 16, unroll=4)
        def _(p):
            state[pl.ds(16 + 2 * p, 2)] = incoming[s, p].astype(F32)

        for layer in range(4):
            d = 2**layer

            @pl.loop(0, 4, unroll=4)
            def _(i):
                base = 40 - 8 * i
                now = state[pl.ds(base, 8)]
                half = taps[3 * layer] * now
                half = half + taps[3 * layer + 1] * state[pl.ds(base - d, 8)]
                half = half + taps[3 * layer + 2] * state[pl.ds(base - 2 * d, 8)]
                squashed = gated(half).astype(BF16)
                pair = [squashed[0:4].reshape(256, 128), squashed[4:8].reshape(256, 128)]
                mixed = dot(mix[layer], jnp.concatenate(pair, axis=1))
                for h in range(2):
                    new = now[4 * h : 4 * h + 4] + mixed[:, 128 * h : 128 * h + 128].reshape(4, 64, 128)
                    if layer < 3:
                        state[pl.ds(base + 4 * h, 4)] = new
                    else:
                        answer[s, pl.ds(12 - 4 * i + 2 * h, 2)] = new.reshape(2, 2, 64, 128).astype(BF16)

    for s in range(2):
        whole(s, incoming.at[s, pl.ds(0, 15)]).wait_recv()
        temporal(s)
        send(2 + s, lambda to, s=s: answer.at[s, to], returned.at[16 * s + me])
        returned[16 * s + me] = answer[s, me]

    for s in range(2):
        whole(2 + s, returned.at[pl.ds(0, 15)]).wait_recv()

    @pl.loop(0, 4, unroll=2)
    def _(pair):
        split = [returned[:, f, pl.ds(16 * pair, 16), :].astype(F32) for f in range(2)]
        for e in range(2):
            g = 2 * pair + e
            both = [part[:, 8 * e : 8 * e + 8].reshape(256, 128) for part in split]
            value = dot(place[...], jnp.concatenate(both, axis=1).astype(BF16))
            for f in range(2):
                for h in range(2):
                    span = slice(128 * h, 128 * h + 128)
                    new = value[256 * h : 256 * h + 256, 128 * f : 128 * f + 128]
                    old = hidden[pl.ds(8 * g, 8), f, :, span].reshape(256, 128).astype(F32)
                    new = jnp.where(covered[:, span] > 0.5, new, old)
                    out_ref[pl.ds(8 * g, 8), f, :, span] = new.reshape(8, 32, 128).astype(BF16)

    for s in range(2):
        whole(s, outgoing.at[pl.ds(0, 15)]).wait_send()
        whole(2 + s, answer.at[s, pl.ds(0, 15)]).wait_send()


def on_device(grid, conv_weight, conv_bias, depth_kernel, point_weight, occupied, counts):
    buffers = [
        ((64, 2, 32, 256), BF16),
        ((16, 768, 256), BF16),
        ((9, 64, 256), F32),
        ((8, 256, 768), BF16),
        ((8, 256, 768), BF16),
        ((256, 256), BF16),
        ((512, 256), BF16),
        ((256, 256), F32),
        ((4, 256, 256), BF16),
        ((12, 64, 128), F32),
        ((64, 256), F32),
        ((256, 256), F32),
        ((256, 128), F32),
        ((256, 128), BF16),
        ((2, 256, 128), BF16),
        ((64, 2, 32, 256), BF16),
        ((32, 2, 64, 128), BF16),
        ((2, 16, 2, 64, 128), BF16),
        ((48, 64, 128), F32),
        ((2, 16, 2, 64, 128), BF16),
        ((32, 2, 64, 128), BF16),
    ]
    return pl.pallas_call(
        kernel,
        out_shape=jax.ShapeDtypeStruct(grid.shape, grid.dtype),
        in_specs=[pl.BlockSpec(memory_space=pltpu.HBM)] * 7,
        out_specs=pl.BlockSpec(memory_space=pltpu.VMEM),
        scratch_shapes=[
            pltpu.VMEM((9, 8, 64), BF16),
            pltpu.VMEM((1, 64), F32),
            pltpu.VMEM((3, 4, 64), F32),
            pltpu.VMEM((4, 64, 64), BF16),
            pltpu.VMEM((1, 32), jnp.int32),
            pltpu.SMEM((1,), jnp.int32),
        ]
        + [pltpu.VMEM(shape, kind) for shape, kind in buffers]
        + [
            pltpu.SemaphoreType.DMA((7,)),
            pltpu.SemaphoreType.DMA((2,)),
            pltpu.SemaphoreType.DMA((2,)),
            pltpu.SemaphoreType.DMA((4,)),
            pltpu.SemaphoreType.DMA((4,)),
        ],
        compiler_params=pltpu.CompilerParams(
            collective_id=0, has_side_effects=True, vmem_limit_bytes=56 * 1024 * 1024
        ),
        cost_estimate=pl.CostEstimate(flops=4_000_000_000, bytes_accessed=4 << 20, transcendentals=3 << 20),
    )(
        grid,
        conv_weight.transpose(0, 2, 1),
        conv_bias.reshape(1, 64),
        depth_kernel.transpose(1, 0, 2),
        point_weight,
        occupied,
        counts,
    )


def solution(mesh):
    placed = (P(None, "frame", None, "tile"), P(), P(), P(), P(), P("tile", None), P("tile"))
    return jax.shard_map(
        on_device,
        mesh=mesh,
        in_specs=placed,
        out_specs=P(None, "frame", None, "tile"),
        check_vma=False,
    )
```

```python
import functools

import jax
import jax.numpy as jnp
from jax import lax
from jax.experimental import pallas as pl
from jax.experimental.pallas import tpu as pltpu
from jax.sharding import PartitionSpec as P

MESH = pl.DeviceIdType.MESH
F32 = jnp.float32
BF16 = jnp.bfloat16
UNROLL = 4

HOPS = (
    (2, 2), (2, 1), (2, 3), (1, 2), (3, 2), (2, 0), (0, 2),
    (1, 1), (3, 3), (1, 3), (3, 1), (1, 0), (3, 0), (0, 1), (0, 3),
)


def rows(shape):
    return lax.broadcasted_iota(jnp.int32, shape, 0)


def cols(shape):
    return lax.broadcasted_iota(jnp.int32, shape, 1)


def one_hot(mask):
    return jnp.where(mask, 1.0, 0.0).astype(BF16)


def dot(lhs, rhs, contract=((1,), (0,))):
    return lax.dot_general(lhs, rhs, (contract, ((), ())), preferred_element_type=F32)


def gated(half):
    return half + half * jnp.tanh(half)


def kernel(
    grid_hbm, weight_hbm, bias_hbm, depth_hbm, point_hbm, occupied_hbm, count_hbm,
    hidden_hbm, returned, place_hbm, covered_hbm,
    weight_ref, bias_ref, depth_ref, point_ref, occupied_ref, count_ref, cells, wide, lanes, band,
    slot_band, pick, place, covered, mix, taps, bias_col, row_col, half_col,
    edge_out, edge_in, hidden, outgoing, incoming, state, answer,
    load_sems, keep_sems, edge_send, edge_recv, send_sems, recv_sems,
):
    me = lax.axis_index("frame")
    tile = lax.axis_index("tile")
    row, col = me // 4, me % 4
    right, left = {"tile": (tile + 1) % 8}, {"tile": (tile + 7) % 8}

    def peer(hop):
        return ((row + hop[0]) % 4) * 4 + (col + hop[1]) % 4

    barrier = pltpu.get_barrier_semaphore()
    for neighbour in (right, left):
        pl.semaphore_signal(barrier, inc=1, device_id=neighbour, device_id_type=MESH)
    for hop in HOPS:
        pl.semaphore_signal(barrier, inc=1, device_id={"frame": peer(hop)}, device_id_type=MESH)
    sources = (grid_hbm, weight_hbm, bias_hbm, depth_hbm, point_hbm, occupied_hbm, count_hbm)
    targets = (cells, weight_ref, bias_ref, depth_ref, point_ref, occupied_ref, count_ref)
    loads = []
    for i, (source, target) in enumerate(zip(sources, targets)):
        loads.append(pltpu.make_async_copy(source, target, load_sems.at[i]))
        loads[i].start()

    loads[0].wait()
    lane, lane_wide = cols((256, 128)), cols((256, 256))
    nought = jnp.zeros((256, 256), BF16)

    def shift(n, edge):
        block = cells[pl.ds(8 * (n // 2), 8), n % 2].reshape(256, 256)
        wide[n, 256:512] = block
        wide[n, 0:256] = jnp.where(lane_wide == 0, nought, pltpu.roll(block, 1, 1))
        wide[n, 512:768] = jnp.where(lane_wide == 255, nought, pltpu.roll(block, 255, 1))
        edge = jnp.where(lane == n, pltpu.roll(block[:, 128:], n + 1, 1), edge)
        return jnp.where(lane == 16 + n, pltpu.roll(block[:, :128], 16 + n, 1), edge)

    edge_out[...] = lax.fori_loop(0, 16, shift, nought[:, :128], unroll=UNROLL)

    for load in loads[1:]:
        load.wait()
    r2, c2 = rows((256, 256)), cols((256, 256))
    listed = occupied_ref[...]
    row_of = (listed >> 1).astype(F32)
    half_of = (listed & 1).astype(F32)
    own = cols((256, 32)) == (rows((256, 32)) >> 3)
    row_here = jnp.sum(jnp.where(own, row_of, 0.0), axis=1, keepdims=True)
    row_col[...] = jnp.broadcast_to(row_here, (256, 256))
    half_col[...] = jnp.broadcast_to(jnp.sum(jnp.where(own, half_of, 0.0), axis=1, keepdims=True), (256, 128))
    pick[...] = one_hot(((r2 & 7) == (c2 >> 5)) & ((c2 & 31).astype(F32) == row_here))
    diagonal = rows((64, 64)) == cols((64, 64))
    bias_half = jnp.sum(jnp.where(diagonal, 0.5 * bias_ref[...], 0.0), axis=1, keepdims=True)
    bias_col[...] = jnp.broadcast_to(bias_half, (64, 256))

    spread = one_hot((cols((8, 256)) >> 5) == rows((8, 256)))
    for tap in range(9):
        lanes[tap] = 0.5 * dot(weight_ref[tap], spread, ((0,), (0,)))
    row_lanes = (cols((8, 256)) & 31).astype(F32)

    @pl.loop(0, 16)
    def _(pair):
        start = pl.multiple_of(16 * pair, 16)
        delta = [row_lanes - row_col[pl.ds(start + 8 * k, 8)] for k in range(2)]
        for g in range(8):
            for dc in range(3):
                parts = []
                for k in range(2):
                    value = jnp.zeros((8, 256), F32)
                    for dr in range(3):
                        value = jnp.where(delta[k] == dr - 1.0, lanes[3 * dr + dc, 8 * g : 8 * g + 8], value)
                    parts.append(value)
                both = jnp.concatenate(parts, axis=0).astype(BF16)
                slot_band[g, pl.ds(start, 16), dc * 256 : (dc + 1) * 256] = both

    pl.semaphore_wait(barrier, 17)
    edge_copies = []
    for side, neighbour in enumerate((right, left)):
        copy = pltpu.make_async_remote_copy(
            src_ref=edge_out,
            dst_ref=edge_in.at[side],
            send_sem=edge_send.at[side],
            recv_sem=edge_recv.at[side],
            device_id=neighbour,
            device_id_type=MESH,
        )
        copy.start()
        edge_copies.append(copy)

    offset = (cols((32, 256)) & 31) - rows((32, 256))

    @pl.loop(0, 8)
    def _(g):
        for dc in range(3):
            for o in range(8):
                value = jnp.zeros((32, 256), F32)
                for dr in range(3):
                    line = lanes[3 * dr + dc, pl.ds(8 * g + o, 1), :]
                    value = jnp.where(offset == dr - 1, line, value)
                band[g, o * 32 : (o + 1) * 32, dc * 256 : (dc + 1) * 256] = value.astype(BF16)

    expand = one_hot((cols((32, 256)) >> 3) == rows((32, 256)))
    row_lane = dot(jnp.broadcast_to(row_of, (8, 32)).astype(BF16), expand)[0:1]
    half_lane = dot(jnp.broadcast_to(half_of, (8, 32)).astype(BF16), expand)[0:1]
    live = (c2 >> 3) < count_ref[0]
    target = ((r2 >> 5) == (c2 & 7)) & ((r2 & 31).astype(F32) == row_lane) & live
    for h in range(2):
        chosen = jnp.where(target & (half_lane == float(h)), 1.0, 0.0)
        place[h * 256 : (h + 1) * 256, :] = chosen.astype(BF16)
        covered[:, h * 128 : (h + 1) * 128] = jnp.broadcast_to(jnp.sum(chosen, axis=1, keepdims=True), (256, 128))

    for layer in range(4):
        for j in range(3):
            line = 0.5 * depth_ref[j, layer : layer + 1, :]
            column = jnp.sum(jnp.where(diagonal, line, 0.0), axis=1, keepdims=True)
            taps[3 * layer + j] = jnp.broadcast_to(column, (64, 128))
    repeat = one_hot((rows((256, 64)) & 63) == cols((256, 64)))
    for layer in range(4):
        tall = dot(repeat, point_ref[layer]).astype(BF16)
        full = dot(tall, repeat, ((1,), (1,)))
        mix[layer] = jnp.where((r2 >> 6) == (c2 >> 6), full, 0.0).astype(BF16)

    for copy in edge_copies:
        copy.wait()
    from_left = jnp.where(tile > 0, edge_in[0], nought[:, :128])
    from_right = jnp.where(tile < 7, edge_in[1], nought[:, :128])

    def fix(n, carry):
        old = wide[n, 0:256, 0:128]
        wide[n, 0:256, 0:128] = jnp.where(lane == 0, pltpu.roll(from_left, (128 - n) % 128, 1), old)
        old = wide[n, 512:768, 128:256]
        wide[n, 512:768, 128:256] = jnp.where(lane == 127, pltpu.roll(from_right, 111 - n, 1), old)
        return carry

    lax.fori_loop(0, 16, fix, 0, unroll=UNROLL)

    def slots(s):
        lo = 128 * s

        @pl.loop(0, 4, unroll=2)
        def _(pair):
            second = half_col[lo : lo + 128] > 0.5
            for f in range(2):
                parts = []
                for e in range(2):
                    g = 2 * pair + e
                    act = dot(slot_band[g, lo : lo + 128, :], wide[2 * g + f])
                    plain = dot(pick[lo : lo + 128, :], wide[2 * g + f, 256:512])
                    act = jnp.where(second, act[:, 128:], act[:, :128]).reshape(16, 8, 128)
                    plain = jnp.where(second, plain[:, 128:], plain[:, :128]).reshape(16, 8, 128)
                    act = act + bias_col[pl.ds(8 * g, 8), 0:128]
                    parts.append(plain + gated(act))
                joined = jnp.concatenate(parts, axis=1).astype(BF16)
                outgoing[16 * s : 16 * s + 16, f, pl.ds(16 * pair, 16), :] = joined

    copies = []

    def send(stage, source, target):
        for hop in HOPS:
            to = peer(hop)
            copy = pltpu.make_async_remote_copy(
                src_ref=source(to),
                dst_ref=target,
                send_sem=send_sems.at[stage],
                recv_sem=recv_sems.at[stage],
                device_id={"frame": to},
                device_id_type=MESH,
            )
            copy.start()

    def whole(stage, ref):
        return pltpu.make_async_remote_copy(
            src_ref=ref,
            dst_ref=ref,
            send_sem=send_sems.at[stage],
            recv_sem=recv_sems.at[stage],
            device_id={"frame": peer(HOPS[0])},
            device_id_type=MESH,
        )

    for s in range(2):
        slots(s)
        send(s, lambda to, s=s: outgoing.at[16 * s + to], incoming.at[s, me])
        incoming[s, me] = outgoing[16 * s + me]

    @pl.loop(0, 8, unroll=2)
    def _(g):
        for f in range(2):
            act = dot(band[g], wide[2 * g + f])
            for o in range(8):
                half = act[o * 32 : (o + 1) * 32] + bias_col[pl.ds(8 * g + o, 1), :]
                value = cells[8 * g + o, f].astype(F32) + gated(half)
                hidden[8 * g + o, f] = value.astype(BF16)

    kept = []

    def keep(source, target):
        copy = pltpu.make_async_copy(source, target, keep_sems.at[len(kept)])
        copy.start()
        kept.append(copy)

    keep(hidden, hidden_hbm)
    keep(place, place_hbm)
    keep(covered, covered_hbm)

    def temporal(s):
        state[0:16] = jnp.zeros((16, 64, 128), F32)

        @pl.loop(0, 16, unroll=4)
        def _(p):
            state[pl.ds(16 + 2 * p, 2)] = incoming[s, p].astype(F32)

        for layer in range(4):
            d = 2**layer

            @pl.loop(0, 4, unroll=4)
            def _(i):
                base = 40 - 8 * i
                now = state[pl.ds(base, 8)]
                half = taps[3 * layer] * now
                half = half + taps[3 * layer + 1] * state[pl.ds(base - d, 8)]
                half = half + taps[3 * layer + 2] * state[pl.ds(base - 2 * d, 8)]
                squashed = gated(half).astype(BF16)
                pair = [squashed[0:4].reshape(256, 128), squashed[4:8].reshape(256, 128)]
                mixed = dot(mix[layer], jnp.concatenate(pair, axis=1))
                for h in range(2):
                    new = now[4 * h : 4 * h + 4] + mixed[:, 128 * h : 128 * h + 128].reshape(4, 64, 128)
                    if layer < 3:
                        state[pl.ds(base + 4 * h, 4)] = new
                    else:
                        answer[s, pl.ds(12 - 4 * i + 2 * h, 2)] = new.reshape(2, 2, 64, 128).astype(BF16)

    for s in range(2):
        whole(s, incoming.at[s, pl.ds(0, 15)]).wait_recv()
        temporal(s)
        send(2 + s, lambda to, s=s: answer.at[s, to], returned.at[16 * s + me])
        keep(answer.at[s, me], returned.at[16 * s + me])

    for s in range(2):
        whole(2 + s, returned.at[pl.ds(0, 15)]).wait_recv()

    for copy in kept:
        copy.wait()
    for s in range(2):
        whole(s, outgoing.at[pl.ds(0, 15)]).wait_send()
        whole(2 + s, answer.at[s, pl.ds(0, 15)]).wait_send()


def merge(hidden_hbm, returned_hbm, place_hbm, covered_hbm, out_hbm, hidden, returned, place, covered, out, in_sems, out_sems):
    loads = [
        pltpu.make_async_copy(place_hbm, place, in_sems.at[8]),
        pltpu.make_async_copy(covered_hbm, covered, in_sems.at[9]),
    ]
    for pair in range(4):
        span = pl.ds(16 * pair, 16)
        source, target = returned_hbm.at[:, :, span], returned.at[:, :, span]
        loads.append(pltpu.make_async_copy(source, target, in_sems.at[2 * pair]))
        loads.append(pltpu.make_async_copy(hidden_hbm.at[span], hidden.at[span], in_sems.at[2 * pair + 1]))
    for load in loads:
        load.start()
    loads[0].wait()
    loads[1].wait()
    stores = []
    for pair in range(4):
        loads[2 + 2 * pair].wait()
        loads[3 + 2 * pair].wait()
        split = [returned[:, f, 16 * pair : 16 * pair + 16, :].astype(F32) for f in range(2)]
        for e in range(2):
            g = 2 * pair + e
            both = [part[:, 8 * e : 8 * e + 8].reshape(256, 128) for part in split]
            value = dot(place[...], jnp.concatenate(both, axis=1).astype(BF16))
            for f in range(2):
                for h in range(2):
                    span = slice(128 * h, 128 * h + 128)
                    new = value[256 * h : 256 * h + 256, 128 * f : 128 * f + 128]
                    old = hidden[8 * g : 8 * g + 8, f, :, span].reshape(256, 128).astype(F32)
                    new = jnp.where(covered[:, span] > 0.5, new, old)
                    out[8 * g : 8 * g + 8, f, :, span] = new.reshape(8, 32, 128).astype(BF16)
        span = pl.ds(16 * pair, 16)
        stores.append(pltpu.make_async_copy(out.at[span], out_hbm.at[span], out_sems.at[pair]))
        stores[pair].start()
    for store in stores:
        store.wait()


def on_device(grid, conv_weight, conv_bias, depth_kernel, point_weight, occupied, counts):
    buffers = [
        ((64, 2, 32, 256), BF16),
        ((16, 768, 256), BF16),
        ((9, 64, 256), F32),
        ((8, 256, 768), BF16),
        ((8, 256, 768), BF16),
        ((256, 256), BF16),
        ((512, 256), BF16),
        ((256, 256), F32),
        ((4, 256, 256), BF16),
        ((12, 64, 128), F32),
        ((64, 256), F32),
        ((256, 256), F32),
        ((256, 128), F32),
        ((256, 128), BF16),
        ((2, 256, 128), BF16),
        ((64, 2, 32, 256), BF16),
        ((32, 2, 64, 128), BF16),
        ((2, 16, 2, 64, 128), BF16),
        ((48, 64, 128), F32),
        ((2, 16, 2, 64, 128), BF16),
    ]
    kinds = [(grid.shape, BF16), ((32, 2, 64, 128), BF16), ((512, 256), BF16), ((256, 256), F32)]
    anywhere = pl.BlockSpec(memory_space=pl.ANY)
    parts = pl.pallas_call(
        kernel,
        out_shape=[jax.ShapeDtypeStruct(shape, kind) for shape, kind in kinds],
        in_specs=[pl.BlockSpec(memory_space=pltpu.HBM)] * 7,
        out_specs=[anywhere] * 4,
        scratch_shapes=[
            pltpu.VMEM((9, 8, 64), BF16),
            pltpu.VMEM((1, 64), F32),
            pltpu.VMEM((3, 4, 64), F32),
            pltpu.VMEM((4, 64, 64), BF16),
            pltpu.VMEM((1, 32), jnp.int32),
            pltpu.SMEM((1,), jnp.int32),
        ]
        + [pltpu.VMEM(shape, kind) for shape, kind in buffers]
        + [
            pltpu.SemaphoreType.DMA((7,)),
            pltpu.SemaphoreType.DMA((5,)),
            pltpu.SemaphoreType.DMA((2,)),
            pltpu.SemaphoreType.DMA((2,)),
            pltpu.SemaphoreType.DMA((4,)),
            pltpu.SemaphoreType.DMA((4,)),
        ],
        compiler_params=pltpu.CompilerParams(
            collective_id=0, has_side_effects=True, vmem_limit_bytes=56 * 1024 * 1024
        ),
        cost_estimate=pl.CostEstimate(flops=4_000_000_000, bytes_accessed=4 << 20, transcendentals=3 << 20),
    )(
        grid,
        conv_weight.transpose(0, 2, 1),
        conv_bias.reshape(1, 64),
        depth_kernel.transpose(1, 0, 2),
        point_weight,
        occupied,
        counts,
    )
    return pl.pallas_call(
        merge,
        out_shape=jax.ShapeDtypeStruct(grid.shape, grid.dtype),
        in_specs=[anywhere] * 4,
        out_specs=anywhere,
        scratch_shapes=[pltpu.VMEM(shape, kind) for shape, kind in kinds]
        + [
            pltpu.VMEM(grid.shape, BF16),
            pltpu.SemaphoreType.DMA((10,)),
            pltpu.SemaphoreType.DMA((4,)),
        ],
        compiler_params=pltpu.CompilerParams(vmem_limit_bytes=56 * 1024 * 1024),
    )(*parts)


def solution(mesh):
    placed = (P(None, "frame", None, "tile"), P(), P(), P(), P(), P("tile", None), P("tile"))
    return jax.shard_map(
        on_device,
        mesh=mesh,
        in_specs=placed,
        out_specs=P(None, "frame", None, "tile"),
        check_vma=False,
    )
```

```python
import functools

import jax
import jax.numpy as jnp
from jax import lax
from jax.experimental import pallas as pl
from jax.experimental.pallas import tpu as pltpu
from jax.sharding import PartitionSpec as P

MESH = pl.DeviceIdType.MESH
F32 = jnp.float32
BF16 = jnp.bfloat16
UNROLL = 4

HOPS = (
    (2, 2), (2, 1), (2, 3), (1, 2), (3, 2), (2, 0), (0, 2),
    (1, 1), (3, 3), (1, 3), (3, 1), (1, 0), (3, 0), (0, 1), (0, 3),
)


def rows(shape):
    return lax.broadcasted_iota(jnp.int32, shape, 0)


def cols(shape):
    return lax.broadcasted_iota(jnp.int32, shape, 1)


def one_hot(mask):
    return jnp.where(mask, 1.0, 0.0).astype(BF16)


def dot(lhs, rhs, contract=((1,), (0,))):
    return lax.dot_general(lhs, rhs, (contract, ((), ())), preferred_element_type=F32)


def gated(half):
    return half + half * jnp.tanh(half)


def kernel(
    grid_hbm, weight_hbm, bias_hbm, depth_hbm, point_hbm, occupied_hbm, count_hbm,
    hidden_hbm, returned, place_hbm, covered_hbm,
    weight_ref, bias_ref, depth_ref, point_ref, occupied_ref, count_ref, cells, wide, lanes, band,
    slot_band, pick, place, covered, mix, taps, bias_col, row_col, half_col,
    edge_out, edge_in, hidden, outgoing, incoming, state, answer,
    load_sems, keep_sems, edge_send, edge_recv, send_sems, recv_sems, row_sem,
):
    me = lax.axis_index("frame")
    tile = lax.axis_index("tile")
    row, col = me // 4, me % 4
    right, left = {"tile": (tile + 1) % 8}, {"tile": (tile + 7) % 8}

    def peer(hop):
        return ((row + hop[0]) % 4) * 4 + (col + hop[1]) % 4

    barrier = pltpu.get_barrier_semaphore()
    for neighbour in (right, left):
        pl.semaphore_signal(barrier, inc=1, device_id=neighbour, device_id_type=MESH)
    for d in (2, 1, 3):
        for hop in ((d, 0), (0, d)):
            pl.semaphore_signal(barrier, inc=1, device_id={"frame": peer(hop)}, device_id_type=MESH)
    sources = (grid_hbm, weight_hbm, bias_hbm, depth_hbm, point_hbm, occupied_hbm, count_hbm)
    targets = (cells, weight_ref, bias_ref, depth_ref, point_ref, occupied_ref, count_ref)
    loads = []
    for i, (source, target) in enumerate(zip(sources, targets)):
        loads.append(pltpu.make_async_copy(source, target, load_sems.at[i]))
        loads[i].start()

    loads[0].wait()
    lane, lane_wide = cols((256, 128)), cols((256, 256))
    nought = jnp.zeros((256, 256), BF16)

    def ends(n, edge):
        block = cells[pl.ds(8 * (n // 2), 8), n % 2].reshape(256, 256)
        edge = jnp.where(lane == n, pltpu.roll(block[:, 128:], n + 1, 1), edge)
        return jnp.where(lane == 16 + n, pltpu.roll(block[:, :128], 16 + n, 1), edge)

    edge_out[...] = lax.fori_loop(0, 16, ends, nought[:, :128], unroll=UNROLL)

    pl.semaphore_wait(barrier, 8)
    edge_copies = []
    for side, neighbour in enumerate((right, left)):
        copy = pltpu.make_async_remote_copy(
            src_ref=edge_out,
            dst_ref=edge_in.at[side],
            send_sem=edge_send.at[side],
            recv_sem=edge_recv.at[side],
            device_id=neighbour,
            device_id_type=MESH,
        )
        copy.start()
        edge_copies.append(copy)

    for d in (2, 1, 3):
        pl.semaphore_signal(row_sem, inc=1, device_id={"frame": peer((0, d))}, device_id_type=MESH)

    def shift(n, carry):
        block = cells[pl.ds(8 * (n // 2), 8), n % 2].reshape(256, 256)
        wide[n, 256:512] = block
        wide[n, 0:256] = jnp.where(lane_wide == 0, nought, pltpu.roll(block, 1, 1))
        wide[n, 512:768] = jnp.where(lane_wide == 255, nought, pltpu.roll(block, 255, 1))
        return carry

    lax.fori_loop(0, 16, shift, 0, unroll=UNROLL)

    for load in loads[1:]:
        load.wait()
    r2, c2 = rows((256, 256)), cols((256, 256))
    listed = occupied_ref[...]
    row_of = (listed >> 1).astype(F32)
    half_of = (listed & 1).astype(F32)
    own = cols((256, 32)) == (rows((256, 32)) >> 3)
    row_here = jnp.sum(jnp.where(own, row_of, 0.0), axis=1, keepdims=True)
    row_col[...] = jnp.broadcast_to(row_here, (256, 256))
    half_col[...] = jnp.broadcast_to(jnp.sum(jnp.where(own, half_of, 0.0), axis=1, keepdims=True), (256, 128))
    pick[...] = one_hot(((r2 & 7) == (c2 >> 5)) & ((c2 & 31).astype(F32) == row_here))
    diagonal = rows((64, 64)) == cols((64, 64))
    bias_half = jnp.sum(jnp.where(diagonal, 0.5 * bias_ref[...], 0.0), axis=1, keepdims=True)
    bias_col[...] = jnp.broadcast_to(bias_half, (64, 256))

    spread = one_hot((cols((8, 256)) >> 5) == rows((8, 256)))
    for tap in range(9):
        lanes[tap] = 0.5 * dot(weight_ref[tap], spread, ((0,), (0,)))
    row_lanes = (cols((8, 256)) & 31).astype(F32)

    @pl.loop(0, 16)
    def _(pair):
        start = pl.multiple_of(16 * pair, 16)
        delta = [row_lanes - row_col[pl.ds(start + 8 * k, 8)] for k in range(2)]
        for g in range(8):
            for dc in range(3):
                parts = []
                for k in range(2):
                    value = jnp.zeros((8, 256), F32)
                    for dr in range(3):
                        value = jnp.where(delta[k] == dr - 1.0, lanes[3 * dr + dc, 8 * g : 8 * g + 8], value)
                    parts.append(value)
                both = jnp.concatenate(parts, axis=0).astype(BF16)
                slot_band[g, pl.ds(start, 16), dc * 256 : (dc + 1) * 256] = both

    for copy in edge_copies:
        copy.wait()
    from_left = jnp.where(tile > 0, edge_in[0], nought[:, :128])
    from_right = jnp.where(tile < 7, edge_in[1], nought[:, :128])

    def fix(n, carry):
        old = wide[n, 0:256, 0:128]
        wide[n, 0:256, 0:128] = jnp.where(lane == 0, pltpu.roll(from_left, (128 - n) % 128, 1), old)
        old = wide[n, 512:768, 128:256]
        wide[n, 512:768, 128:256] = jnp.where(lane == 127, pltpu.roll(from_right, 111 - n, 1), old)
        return carry

    lax.fori_loop(0, 16, fix, 0, unroll=UNROLL)

    def slots(s):
        lo = 128 * s

        @pl.loop(0, 4, unroll=2)
        def _(pair):
            second = half_col[lo : lo + 128] > 0.5
            for f in range(2):
                parts = []
                for e in range(2):
                    g = 2 * pair + e
                    act = dot(slot_band[g, lo : lo + 128, :], wide[2 * g + f])
                    plain = dot(pick[lo : lo + 128, :], wide[2 * g + f, 256:512])
                    act = jnp.where(second, act[:, 128:], act[:, :128]).reshape(16, 8, 128)
                    plain = jnp.where(second, plain[:, 128:], plain[:, :128]).reshape(16, 8, 128)
                    act = act + bias_col[pl.ds(8 * g, 8), 0:128]
                    parts.append(plain + gated(act))
                joined = jnp.concatenate(parts, axis=1).astype(BF16)
                outgoing[16 * s : 16 * s + 16, f, pl.ds(16 * pair, 16), :] = joined

    copies = []

    def send(stage, source, target):
        for hop in HOPS:
            to = peer(hop)
            copy = pltpu.make_async_remote_copy(
                src_ref=source(to),
                dst_ref=target,
                send_sem=send_sems.at[stage],
                recv_sem=recv_sems.at[stage],
                device_id={"frame": to},
                device_id_type=MESH,
            )
            copy.start()

    def whole(stage, ref):
        return pltpu.make_async_remote_copy(
            src_ref=ref,
            dst_ref=ref,
            send_sem=send_sems.at[stage],
            recv_sem=recv_sems.at[stage],
            device_id={"frame": peer(HOPS[0])},
            device_id_type=MESH,
        )

    for s in range(2):
        slots(s)
        if s == 0:
            pl.semaphore_wait(row_sem, 3)
        else:
            whole(0, outgoing.at[pl.ds(0, 15)]).wait_send()
        send(s, lambda to, s=s: outgoing.at[16 * s + to], incoming.at[s, me])
        incoming[s, me] = outgoing[16 * s + me]

    offset = (cols((32, 256)) & 31) - rows((32, 256))

    @pl.loop(0, 8)
    def _(g):
        for dc in range(3):
            for o in range(8):
                value = jnp.zeros((32, 256), F32)
                for dr in range(3):
                    line = lanes[3 * dr + dc, pl.ds(8 * g + o, 1), :]
                    value = jnp.where(offset == dr - 1, line, value)
                band[g, o * 32 : (o + 1) * 32, dc * 256 : (dc + 1) * 256] = value.astype(BF16)

    expand = one_hot((cols((32, 256)) >> 3) == rows((32, 256)))
    row_lane = dot(jnp.broadcast_to(row_of, (8, 32)).astype(BF16), expand)[0:1]
    half_lane = dot(jnp.broadcast_to(half_of, (8, 32)).astype(BF16), expand)[0:1]
    live = (c2 >> 3) < count_ref[0]
    target = ((r2 >> 5) == (c2 & 7)) & ((r2 & 31).astype(F32) == row_lane) & live
    for h in range(2):
        chosen = jnp.where(target & (half_lane == float(h)), 1.0, 0.0)
        place[h * 256 : (h + 1) * 256, :] = chosen.astype(BF16)
        covered[:, h * 128 : (h + 1) * 128] = jnp.broadcast_to(jnp.sum(chosen, axis=1, keepdims=True), (256, 128))

    for layer in range(4):
        for j in range(3):
            line = 0.5 * depth_ref[j, layer : layer + 1, :]
            column = jnp.sum(jnp.where(diagonal, line, 0.0), axis=1, keepdims=True)
            taps[3 * layer + j] = jnp.broadcast_to(column, (64, 128))
    repeat = one_hot((rows((256, 64)) & 63) == cols((256, 64)))
    for layer in range(4):
        tall = dot(repeat, point_ref[layer]).astype(BF16)
        full = dot(tall, repeat, ((1,), (1,)))
        mix[layer] = jnp.where((r2 >> 6) == (c2 >> 6), full, 0.0).astype(BF16)

    @pl.loop(0, 8, unroll=2)
    def _(g):
        for f in range(2):
            act = dot(band[g], wide[2 * g + f])
            for o in range(8):
                half = act[o * 32 : (o + 1) * 32] + bias_col[pl.ds(8 * g + o, 1), :]
                value = cells[8 * g + o, f].astype(F32) + gated(half)
                hidden[8 * g + o, f] = value.astype(BF16)

    kept = []

    def keep(source, target):
        copy = pltpu.make_async_copy(source, target, keep_sems.at[len(kept)])
        copy.start()
        kept.append(copy)

    keep(hidden, hidden_hbm)
    keep(place, place_hbm)
    keep(covered, covered_hbm)

    def temporal(s):
        state[0:16] = jnp.zeros((16, 64, 128), F32)

        @pl.loop(0, 16, unroll=4)
        def _(p):
            state[pl.ds(16 + 2 * p, 2)] = incoming[s, p].astype(F32)

        for layer in range(4):
            d = 2**layer

            @pl.loop(0, 4, unroll=4)
            def _(i):
                base = 40 - 8 * i
                now = state[pl.ds(base, 8)]
                half = taps[3 * layer] * now
                half = half + taps[3 * layer + 1] * state[pl.ds(base - d, 8)]
                half = half + taps[3 * layer + 2] * state[pl.ds(base - 2 * d, 8)]
                squashed = gated(half).astype(BF16)
                pair = [squashed[0:4].reshape(256, 128), squashed[4:8].reshape(256, 128)]
                mixed = dot(mix[layer], jnp.concatenate(pair, axis=1))
                for h in range(2):
                    new = now[4 * h : 4 * h + 4] + mixed[:, 128 * h : 128 * h + 128].reshape(4, 64, 128)
                    if layer < 3:
                        state[pl.ds(base + 4 * h, 4)] = new
                    else:
                        answer[s, pl.ds(12 - 4 * i + 2 * h, 2)] = new.reshape(2, 2, 64, 128).astype(BF16)

    for s in range(2):
        whole(s, incoming.at[s, pl.ds(0, 15)]).wait_recv()
        temporal(s)
        send(2 + s, lambda to, s=s: answer.at[s, to], returned.at[16 * s + me])
        keep(answer.at[s, me], returned.at[16 * s + me])

    for s in range(2):
        whole(2 + s, returned.at[pl.ds(0, 15)]).wait_recv()

    for copy in kept:
        copy.wait()
    for s in range(2):
        if s:
            whole(s, outgoing.at[pl.ds(0, 15)]).wait_send()
        whole(2 + s, answer.at[s, pl.ds(0, 15)]).wait_send()


def merge(hidden_hbm, returned_hbm, place_hbm, covered_hbm, out_hbm, hidden, returned, place, covered, out, in_sems, out_sems):
    loads = [
        pltpu.make_async_copy(place_hbm, place, in_sems.at[8]),
        pltpu.make_async_copy(covered_hbm, covered, in_sems.at[9]),
    ]
    for pair in range(4):
        span = pl.ds(16 * pair, 16)
        source, target = returned_hbm.at[:, :, span], returned.at[:, :, span]
        loads.append(pltpu.make_async_copy(source, target, in_sems.at[2 * pair]))
        loads.append(pltpu.make_async_copy(hidden_hbm.at[span], hidden.at[span], in_sems.at[2 * pair + 1]))
    for load in loads:
        load.start()
    loads[0].wait()
    loads[1].wait()
    stores = []
    for pair in range(4):
        loads[2 + 2 * pair].wait()
        loads[3 + 2 * pair].wait()
        split = [returned[:, f, 16 * pair : 16 * pair + 16, :].astype(F32) for f in range(2)]
        for e in range(2):
            g = 2 * pair + e
            both = [part[:, 8 * e : 8 * e + 8].reshape(256, 128) for part in split]
            value = dot(place[...], jnp.concatenate(both, axis=1).astype(BF16))
            for f in range(2):
                for h in range(2):
                    span = slice(128 * h, 128 * h + 128)
                    new = value[256 * h : 256 * h + 256, 128 * f : 128 * f + 128]
                    old = hidden[8 * g : 8 * g + 8, f, :, span].reshape(256, 128).astype(F32)
                    new = jnp.where(covered[:, span] > 0.5, new, old)
                    out[8 * g : 8 * g + 8, f, :, span] = new.reshape(8, 32, 128).astype(BF16)
        span = pl.ds(16 * pair, 16)
        stores.append(pltpu.make_async_copy(out.at[span], out_hbm.at[span], out_sems.at[pair]))
        stores[pair].start()
    for store in stores:
        store.wait()


def on_device(grid, conv_weight, conv_bias, depth_kernel, point_weight, occupied, counts):
    buffers = [
        ((64, 2, 32, 256), BF16),
        ((16, 768, 256), BF16),
        ((9, 64, 256), F32),
        ((8, 256, 768), BF16),
        ((8, 256, 768), BF16),
        ((256, 256), BF16),
        ((512, 256), BF16),
        ((256, 256), F32),
        ((4, 256, 256), BF16),
        ((12, 64, 128), F32),
        ((64, 256), F32),
        ((256, 256), F32),
        ((256, 128), F32),
        ((256, 128), BF16),
        ((2, 256, 128), BF16),
        ((64, 2, 32, 256), BF16),
        ((32, 2, 64, 128), BF16),
        ((2, 16, 2, 64, 128), BF16),
        ((48, 64, 128), F32),
        ((2, 16, 2, 64, 128), BF16),
    ]
    kinds = [(grid.shape, BF16), ((32, 2, 64, 128), BF16), ((512, 256), BF16), ((256, 256), F32)]
    anywhere = pl.BlockSpec(memory_space=pl.ANY)
    parts = pl.pallas_call(
        kernel,
        out_shape=[jax.ShapeDtypeStruct(shape, kind) for shape, kind in kinds],
        in_specs=[pl.BlockSpec(memory_space=pltpu.HBM)] * 7,
        out_specs=[anywhere] * 4,
        scratch_shapes=[
            pltpu.VMEM((9, 8, 64), BF16),
            pltpu.VMEM((1, 64), F32),
            pltpu.VMEM((3, 4, 64), F32),
            pltpu.VMEM((4, 64, 64), BF16),
            pltpu.VMEM((1, 32), jnp.int32),
            pltpu.SMEM((1,), jnp.int32),
        ]
        + [pltpu.VMEM(shape, kind) for shape, kind in buffers]
        + [
            pltpu.SemaphoreType.DMA((7,)),
            pltpu.SemaphoreType.DMA((5,)),
            pltpu.SemaphoreType.DMA((2,)),
            pltpu.SemaphoreType.DMA((2,)),
            pltpu.SemaphoreType.DMA((4,)),
            pltpu.SemaphoreType.DMA((4,)),
            pltpu.SemaphoreType.REGULAR,
        ],
        compiler_params=pltpu.CompilerParams(
            collective_id=0, has_side_effects=True, vmem_limit_bytes=56 * 1024 * 1024
        ),
        cost_estimate=pl.CostEstimate(flops=4_000_000_000, bytes_accessed=4 << 20, transcendentals=3 << 20),
    )(
        grid,
        conv_weight.transpose(0, 2, 1),
        conv_bias.reshape(1, 64),
        depth_kernel.transpose(1, 0, 2),
        point_weight,
        occupied,
        counts,
    )
    return pl.pallas_call(
        merge,
        out_shape=jax.ShapeDtypeStruct(grid.shape, grid.dtype),
        in_specs=[anywhere] * 4,
        out_specs=anywhere,
        scratch_shapes=[pltpu.VMEM(shape, kind) for shape, kind in kinds]
        + [
            pltpu.VMEM(grid.shape, BF16),
            pltpu.SemaphoreType.DMA((10,)),
            pltpu.SemaphoreType.DMA((4,)),
        ],
        compiler_params=pltpu.CompilerParams(vmem_limit_bytes=56 * 1024 * 1024),
    )(*parts)


def solution(mesh):
    placed = (P(None, "frame", None, "tile"), P(), P(), P(), P(), P("tile", None), P("tile"))
    return jax.shard_map(
        on_device,
        mesh=mesh,
        in_specs=placed,
        out_specs=P(None, "frame", None, "tile"),
        check_vma=False,
    )
```

```python
import functools

import jax
import jax.numpy as jnp
from jax import lax
from jax.experimental import pallas as pl
from jax.experimental.pallas import tpu as pltpu
from jax.sharding import PartitionSpec as P

MESH = pl.DeviceIdType.MESH
F32 = jnp.float32
BF16 = jnp.bfloat16
UNROLL = 4

HOPS = (
    (2, 2), (2, 1), (2, 3), (1, 2), (3, 2), (2, 0), (0, 2),
    (1, 1), (3, 3), (1, 3), (3, 1), (1, 0), (3, 0), (0, 1), (0, 3),
)


def rows(shape):
    return lax.broadcasted_iota(jnp.int32, shape, 0)


def cols(shape):
    return lax.broadcasted_iota(jnp.int32, shape, 1)


def one_hot(mask):
    return jnp.where(mask, 1.0, 0.0).astype(BF16)


def dot(lhs, rhs, contract=((1,), (0,))):
    return lax.dot_general(lhs, rhs, (contract, ((), ())), preferred_element_type=F32)


def gated(half):
    return half + half * jnp.tanh(half)


def kernel(
    grid_hbm, weight_hbm, bias_hbm, depth_hbm, point_hbm, occupied_hbm, count_hbm,
    out_ref,
    weight_ref, bias_ref, depth_ref, point_ref, occupied_ref, count_ref, cells, wide, lanes, band,
    slot_band, pick, place, covered, mix, taps, bias_col, row_col, half_col,
    edge_out, edge_in, outgoing, incoming, state, answer, returned,
    load_sems, edge_send, edge_recv, send_sems, recv_sems, row_sem,
):
    me = lax.axis_index("frame")
    tile = lax.axis_index("tile")
    row, col = me // 4, me % 4
    right, left = {"tile": (tile + 1) % 8}, {"tile": (tile + 7) % 8}

    def peer(hop):
        return ((row + hop[0]) % 4) * 4 + (col + hop[1]) % 4

    barrier = pltpu.get_barrier_semaphore()
    for neighbour in (right, left):
        pl.semaphore_signal(barrier, inc=1, device_id=neighbour, device_id_type=MESH)
    for d in (2, 1, 3):
        for hop in ((d, 0), (0, d)):
            pl.semaphore_signal(barrier, inc=1, device_id={"frame": peer(hop)}, device_id_type=MESH)
    sources = (grid_hbm, weight_hbm, bias_hbm, depth_hbm, point_hbm, occupied_hbm, count_hbm)
    targets = (cells, weight_ref, bias_ref, depth_ref, point_ref, occupied_ref, count_ref)
    loads = []
    for i, (source, target) in enumerate(zip(sources, targets)):
        loads.append(pltpu.make_async_copy(source, target, load_sems.at[i]))
        loads[i].start()

    loads[0].wait()
    lane, lane_wide = cols((256, 128)), cols((256, 256))
    nought = jnp.zeros((256, 256), BF16)

    def ends(n, edge):
        block = cells[pl.ds(8 * (n // 2), 8), n % 2].reshape(256, 256)
        edge = jnp.where(lane == n, pltpu.roll(block[:, 128:], n + 1, 1), edge)
        return jnp.where(lane == 16 + n, pltpu.roll(block[:, :128], 16 + n, 1), edge)

    edge_out[...] = lax.fori_loop(0, 16, ends, nought[:, :128], unroll=UNROLL)

    pl.semaphore_wait(barrier, 8)
    edge_copies = []
    for side, neighbour in enumerate((right, left)):
        copy = pltpu.make_async_remote_copy(
            src_ref=edge_out,
            dst_ref=edge_in.at[side],
            send_sem=edge_send.at[side],
            recv_sem=edge_recv.at[side],
            device_id=neighbour,
            device_id_type=MESH,
        )
        copy.start()
        edge_copies.append(copy)

    for d in (2, 1, 3):
        pl.semaphore_signal(row_sem, inc=1, device_id={"frame": peer((0, d))}, device_id_type=MESH)

    def shift(n, carry):
        block = cells[pl.ds(8 * (n // 2), 8), n % 2].reshape(256, 256)
        wide[n, 256:512] = block
        wide[n, 0:256] = jnp.where(lane_wide == 0, nought, pltpu.roll(block, 1, 1))
        wide[n, 512:768] = jnp.where(lane_wide == 255, nought, pltpu.roll(block, 255, 1))
        return carry

    lax.fori_loop(0, 16, shift, 0, unroll=UNROLL)

    for load in loads[1:]:
        load.wait()
    r2, c2 = rows((256, 256)), cols((256, 256))
    listed = occupied_ref[...]
    row_of = (listed >> 1).astype(F32)
    half_of = (listed & 1).astype(F32)
    own = cols((256, 32)) == (rows((256, 32)) >> 3)
    row_here = jnp.sum(jnp.where(own, row_of, 0.0), axis=1, keepdims=True)
    row_col[...] = jnp.broadcast_to(row_here, (256, 256))
    half_col[...] = jnp.broadcast_to(jnp.sum(jnp.where(own, half_of, 0.0), axis=1, keepdims=True), (256, 128))
    pick[...] = one_hot(((r2 & 7) == (c2 >> 5)) & ((c2 & 31).astype(F32) == row_here))
    diagonal = rows((64, 64)) == cols((64, 64))
    bias_half = jnp.sum(jnp.where(diagonal, 0.5 * bias_ref[...], 0.0), axis=1, keepdims=True)
    bias_col[...] = jnp.broadcast_to(bias_half, (64, 256))

    spread = one_hot((cols((8, 256)) >> 5) == rows((8, 256)))
    for tap in range(9):
        lanes[tap] = 0.5 * dot(weight_ref[tap], spread, ((0,), (0,)))
    row_lanes = (cols((8, 256)) & 31).astype(F32)

    @pl.loop(0, 16)
    def _(pair):
        start = pl.multiple_of(16 * pair, 16)
        delta = [row_lanes - row_col[pl.ds(start + 8 * k, 8)] for k in range(2)]
        for g in range(8):
            for dc in range(3):
                parts = []
                for k in range(2):
                    value = jnp.zeros((8, 256), F32)
                    for dr in range(3):
                        value = jnp.where(delta[k] == dr - 1.0, lanes[3 * dr + dc, 8 * g : 8 * g + 8], value)
                    parts.append(value)
                both = jnp.concatenate(parts, axis=0).astype(BF16)
                slot_band[g, pl.ds(start, 16), dc * 256 : (dc + 1) * 256] = both

    for copy in edge_copies:
        copy.wait()
    from_left = jnp.where(tile > 0, edge_in[0], nought[:, :128])
    from_right = jnp.where(tile < 7, edge_in[1], nought[:, :128])

    def fix(n, carry):
        old = wide[n, 0:256, 0:128]
        wide[n, 0:256, 0:128] = jnp.where(lane == 0, pltpu.roll(from_left, (128 - n) % 128, 1), old)
        old = wide[n, 512:768, 128:256]
        wide[n, 512:768, 128:256] = jnp.where(lane == 127, pltpu.roll(from_right, 111 - n, 1), old)
        return carry

    lax.fori_loop(0, 16, fix, 0, unroll=UNROLL)

    def slots(s):
        lo = 128 * s

        @pl.loop(0, 4, unroll=2)
        def _(pair):
            second = half_col[lo : lo + 128] > 0.5
            for f in range(2):
                parts = []
                for e in range(2):
                    g = 2 * pair + e
                    act = dot(slot_band[g, lo : lo + 128, :], wide[2 * g + f])
                    plain = dot(pick[lo : lo + 128, :], wide[2 * g + f, 256:512])
                    act = jnp.where(second, act[:, 128:], act[:, :128]).reshape(16, 8, 128)
                    plain = jnp.where(second, plain[:, 128:], plain[:, :128]).reshape(16, 8, 128)
                    act = act + bias_col[pl.ds(8 * g, 8), 0:128]
                    parts.append(plain + gated(act))
                joined = jnp.concatenate(parts, axis=1).astype(BF16)
                outgoing[16 * s : 16 * s + 16, f, pl.ds(16 * pair, 16), :] = joined

    copies = []

    def send(stage, source, target):
        for hop in HOPS:
            to = peer(hop)
            copy = pltpu.make_async_remote_copy(
                src_ref=source(to),
                dst_ref=target,
                send_sem=send_sems.at[stage],
                recv_sem=recv_sems.at[stage],
                device_id={"frame": to},
                device_id_type=MESH,
            )
            copy.start()

    def whole(stage, ref):
        return pltpu.make_async_remote_copy(
            src_ref=ref,
            dst_ref=ref,
            send_sem=send_sems.at[stage],
            recv_sem=recv_sems.at[stage],
            device_id={"frame": peer(HOPS[0])},
            device_id_type=MESH,
        )

    for s in range(2):
        slots(s)
        if s == 0:
            pl.semaphore_wait(row_sem, 3)
        else:
            whole(0, outgoing.at[pl.ds(0, 15)]).wait_send()
        send(s, lambda to, s=s: outgoing.at[16 * s + to], incoming.at[s, me])
        incoming[s, me] = outgoing[16 * s + me]

    offset = (cols((32, 256)) & 31) - rows((32, 256))

    @pl.loop(0, 8)
    def _(g):
        for dc in range(3):
            for o in range(8):
                value = jnp.zeros((32, 256), F32)
                for dr in range(3):
                    line = lanes[3 * dr + dc, pl.ds(8 * g + o, 1), :]
                    value = jnp.where(offset == dr - 1, line, value)
                band[g, o * 32 : (o + 1) * 32, dc * 256 : (dc + 1) * 256] = value.astype(BF16)

    expand = one_hot((cols((32, 256)) >> 3) == rows((32, 256)))
    row_lane = dot(jnp.broadcast_to(row_of, (8, 32)).astype(BF16), expand)[0:1]
    half_lane = dot(jnp.broadcast_to(half_of, (8, 32)).astype(BF16), expand)[0:1]
    live = (c2 >> 3) < count_ref[0]
    target = ((r2 >> 5) == (c2 & 7)) & ((r2 & 31).astype(F32) == row_lane) & live
    for h in range(2):
        chosen = jnp.where(target & (half_lane == float(h)), 1.0, 0.0)
        place[h * 256 : (h + 1) * 256, :] = chosen.astype(BF16)
        for s in range(2):
            found = jnp.sum(chosen[:, 128 * s : 128 * s + 128], axis=1, keepdims=True)
            covered[s, :, h * 128 : (h + 1) * 128] = jnp.broadcast_to(found, (256, 128))

    for layer in range(4):
        for j in range(3):
            line = 0.5 * depth_ref[j, layer : layer + 1, :]
            column = jnp.sum(jnp.where(diagonal, line, 0.0), axis=1, keepdims=True)
            taps[3 * layer + j] = jnp.broadcast_to(column, (64, 128))
    repeat = one_hot((rows((256, 64)) & 63) == cols((256, 64)))
    for layer in range(4):
        tall = dot(repeat, point_ref[layer]).astype(BF16)
        full = dot(tall, repeat, ((1,), (1,)))
        mix[layer] = jnp.where((r2 >> 6) == (c2 >> 6), full, 0.0).astype(BF16)

    @pl.loop(0, 8, unroll=2)
    def _(g):
        for f in range(2):
            act = dot(band[g], wide[2 * g + f])
            for o in range(8):
                half = act[o * 32 : (o + 1) * 32] + bias_col[pl.ds(8 * g + o, 1), :]
                value = cells[8 * g + o, f].astype(F32) + gated(half)
                out_ref[8 * g + o, f] = value.astype(BF16)

    def temporal(s):
        state[0:16] = jnp.zeros((16, 64, 128), F32)

        @pl.loop(0, 16, unroll=4)
        def _(p):
            state[pl.ds(16 + 2 * p, 2)] = incoming[s, p].astype(F32)

        for layer in range(4):
            d = 2**layer

            @pl.loop(0, 4, unroll=4)
            def _(i):
                base = 40 - 8 * i
                now = state[pl.ds(base, 8)]
                half = taps[3 * layer] * now
                half = half + taps[3 * layer + 1] * state[pl.ds(base - d, 8)]
                half = half + taps[3 * layer + 2] * state[pl.ds(base - 2 * d, 8)]
                squashed = gated(half).astype(BF16)
                pair = [squashed[0:4].reshape(256, 128), squashed[4:8].reshape(256, 128)]
                mixed = dot(mix[layer], jnp.concatenate(pair, axis=1))
                for h in range(2):
                    new = now[4 * h : 4 * h + 4] + mixed[:, 128 * h : 128 * h + 128].reshape(4, 64, 128)
                    if layer < 3:
                        state[pl.ds(base + 4 * h, 4)] = new
                    else:
                        answer[s, pl.ds(12 - 4 * i + 2 * h, 2)] = new.reshape(2, 2, 64, 128).astype(BF16)

    for s in range(2):
        whole(s, incoming.at[s, pl.ds(0, 15)]).wait_recv()
        temporal(s)
        send(2 + s, lambda to, s=s: answer.at[s, to], returned.at[16 * s + me])
        returned[16 * s + me] = answer[s, me]

    def merge(s):
        @pl.loop(0, 4, unroll=2)
        def _(pair):
            split = [returned[16 * s : 16 * s + 16, f, pl.ds(16 * pair, 16), :].astype(F32) for f in range(2)]
            for e in range(2):
                g = 2 * pair + e
                both = [part[:, 8 * e : 8 * e + 8].reshape(128, 128) for part in split]
                value = dot(place[:, 128 * s : 128 * s + 128], jnp.concatenate(both, axis=1).astype(BF16))
                for f in range(2):
                    for h in range(2):
                        span = slice(128 * h, 128 * h + 128)
                        new = value[256 * h : 256 * h + 256, 128 * f : 128 * f + 128]
                        old = out_ref[pl.ds(8 * g, 8), f, :, span].reshape(256, 128).astype(F32)
                        new = jnp.where(covered[s, :, span] > 0.5, new, old)
                        out_ref[pl.ds(8 * g, 8), f, :, span] = new.reshape(8, 32, 128).astype(BF16)

    for s in range(2):
        whole(2 + s, returned.at[pl.ds(0, 15)]).wait_recv()
        merge(s)

    for s in range(2):
        if s:
            whole(s, outgoing.at[pl.ds(0, 15)]).wait_send()
        whole(2 + s, answer.at[s, pl.ds(0, 15)]).wait_send()


def on_device(grid, conv_weight, conv_bias, depth_kernel, point_weight, occupied, counts):
    buffers = [
        ((64, 2, 32, 256), BF16),
        ((16, 768, 256), BF16),
        ((9, 64, 256), F32),
        ((8, 256, 768), BF16),
        ((8, 256, 768), BF16),
        ((256, 256), BF16),
        ((512, 256), BF16),
        ((2, 256, 256), F32),
        ((4, 256, 256), BF16),
        ((12, 64, 128), F32),
        ((64, 256), F32),
        ((256, 256), F32),
        ((256, 128), F32),
        ((256, 128), BF16),
        ((2, 256, 128), BF16),
        ((32, 2, 64, 128), BF16),
        ((2, 16, 2, 64, 128), BF16),
        ((48, 64, 128), F32),
        ((2, 16, 2, 64, 128), BF16),
        ((32, 2, 64, 128), BF16),
    ]
    return pl.pallas_call(
        kernel,
        out_shape=jax.ShapeDtypeStruct(grid.shape, grid.dtype),
        in_specs=[pl.BlockSpec(memory_space=pltpu.HBM)] * 7,
        out_specs=pl.BlockSpec(memory_space=pltpu.VMEM),
        scratch_shapes=[
            pltpu.VMEM((9, 8, 64), BF16),
            pltpu.VMEM((1, 64), F32),
            pltpu.VMEM((3, 4, 64), F32),
            pltpu.VMEM((4, 64, 64), BF16),
            pltpu.VMEM((1, 32), jnp.int32),
            pltpu.SMEM((1,), jnp.int32),
        ]
        + [pltpu.VMEM(shape, kind) for shape, kind in buffers]
        + [
            pltpu.SemaphoreType.DMA((7,)),
            pltpu.SemaphoreType.DMA((2,)),
            pltpu.SemaphoreType.DMA((2,)),
            pltpu.SemaphoreType.DMA((4,)),
            pltpu.SemaphoreType.DMA((4,)),
            pltpu.SemaphoreType.REGULAR,
        ],
        compiler_params=pltpu.CompilerParams(
            collective_id=0, has_side_effects=True, vmem_limit_bytes=36 * 1024 * 1024
        ),
        cost_estimate=pl.CostEstimate(flops=4_000_000_000, bytes_accessed=0, transcendentals=3 << 20),
    )(
        *(
            pltpu.with_memory_space_constraint(array, pltpu.HBM)
            for array in (
                grid,
                conv_weight.transpose(0, 2, 1),
                conv_bias.reshape(1, 64),
                depth_kernel.transpose(1, 0, 2),
                point_weight,
                occupied,
            )
        ),
        counts,
    )


def solution(mesh):
    placed = (P(None, "frame", None, "tile"), P(), P(), P(), P(), P("tile", None), P("tile"))
    return jax.shard_map(
        on_device,
        mesh=mesh,
        in_specs=placed,
        out_specs=P(None, "frame", None, "tile"),
        check_vma=False,
    )
```

```python
import functools

import jax
import jax.numpy as jnp
from jax import lax
from jax.experimental import pallas as pl
from jax.experimental.pallas import tpu as pltpu
from jax.sharding import PartitionSpec as P

MESH = pl.DeviceIdType.MESH
F32 = jnp.float32
BF16 = jnp.bfloat16
UNROLL = 16

HOPS = (
    (2, 2), (2, 1), (2, 3), (1, 2), (3, 2), (2, 0), (0, 2),
    (1, 1), (3, 3), (1, 3), (3, 1), (1, 0), (3, 0), (0, 1), (0, 3),
)


def rows(shape):
    return lax.broadcasted_iota(jnp.int32, shape, 0)


def cols(shape):
    return lax.broadcasted_iota(jnp.int32, shape, 1)


def one_hot(mask):
    return jnp.where(mask, 1.0, 0.0).astype(BF16)


def dot(lhs, rhs, contract=((1,), (0,))):
    return lax.dot_general(lhs, rhs, (contract, ((), ())), preferred_element_type=F32)


def gated(half):
    return half + half * jnp.tanh(half)


def kernel(
    grid_hbm, weight_hbm, bias_hbm, depth_hbm, point_hbm, occupied_hbm, count_hbm,
    out_ref,
    weight_ref, bias_ref, depth_ref, point_ref, occupied_ref, count_ref, cells, wide, lanes, band,
    slot_band, pick, place, covered, mix, taps, bias_col, row_col, half_col,
    edge_out, edge_in, outgoing, incoming, state, answer, returned,
    load_sems, edge_send, edge_recv, send_sems, recv_sems, row_sem,
):
    me = lax.axis_index("frame")
    tile = lax.axis_index("tile")
    row, col = me // 4, me % 4
    right, left = {"tile": (tile + 1) % 8}, {"tile": (tile + 7) % 8}

    def peer(hop):
        return ((row + hop[0]) % 4) * 4 + (col + hop[1]) % 4

    barrier = pltpu.get_barrier_semaphore()
    for neighbour in (right, left):
        pl.semaphore_signal(barrier, inc=1, device_id=neighbour, device_id_type=MESH)
    for d in (2, 1, 3):
        for hop in ((d, 0), (0, d)):
            pl.semaphore_signal(barrier, inc=1, device_id={"frame": peer(hop)}, device_id_type=MESH)
    sources = (weight_hbm, bias_hbm, depth_hbm, point_hbm, occupied_hbm, count_hbm)
    targets = (weight_ref, bias_ref, depth_ref, point_ref, occupied_ref, count_ref)
    quarters = []
    for i in range(4):
        span = pl.ds(16 * i, 16)
        quarters.append(pltpu.make_async_copy(grid_hbm.at[span], cells.at[span], load_sems.at[7 + i]))
        quarters[i].start()
    loads = []
    for i, (source, target) in enumerate(zip(sources, targets)):
        loads.append(pltpu.make_async_copy(source, target, load_sems.at[i]))
        loads[i].start()

    lane, lane_wide = cols((256, 128)), cols((256, 256))
    nought = jnp.zeros((256, 256), BF16)

    def ends(n, edge):
        block = cells[pl.ds(8 * (n // 2), 8), n % 2].reshape(256, 256)
        edge = jnp.where(lane == n, pltpu.roll(block[:, 128:], n + 1, 1), edge)
        return jnp.where(lane == 16 + n, pltpu.roll(block[:, :128], 16 + n, 1), edge)

    edge = nought[:, :128]
    for i in range(4):
        quarters[i].wait()
        edge = lax.fori_loop(4 * i, 4 * i + 4, ends, edge, unroll=4)
    edge_out[...] = edge

    pl.semaphore_wait(barrier, 8)
    edge_copies = []
    for side, neighbour in enumerate((right, left)):
        copy = pltpu.make_async_remote_copy(
            src_ref=edge_out,
            dst_ref=edge_in.at[side],
            send_sem=edge_send.at[side],
            recv_sem=edge_recv.at[side],
            device_id=neighbour,
            device_id_type=MESH,
        )
        copy.start()
        edge_copies.append(copy)

    for d in (2, 1, 3):
        pl.semaphore_signal(row_sem, inc=1, device_id={"frame": peer((0, d))}, device_id_type=MESH)

    def shift(n, carry):
        block = cells[pl.ds(8 * (n // 2), 8), n % 2].reshape(256, 256)
        wide[n, 256:512] = block
        wide[n, 0:256] = jnp.where(lane_wide == 0, nought, pltpu.roll(block, 1, 1))
        wide[n, 512:768] = jnp.where(lane_wide == 255, nought, pltpu.roll(block, 255, 1))
        return carry

    lax.fori_loop(0, 16, shift, 0, unroll=UNROLL)

    for load in loads:
        load.wait()
    r2, c2 = rows((256, 256)), cols((256, 256))
    listed = occupied_ref[...]
    row_of = (listed >> 1).astype(F32)
    half_of = (listed & 1).astype(F32)
    own = cols((256, 32)) == (rows((256, 32)) >> 3)
    row_here = jnp.sum(jnp.where(own, row_of, 0.0), axis=1, keepdims=True)
    row_col[...] = jnp.broadcast_to(row_here, (256, 256))
    half_col[...] = jnp.broadcast_to(jnp.sum(jnp.where(own, half_of, 0.0), axis=1, keepdims=True), (256, 128))
    pick[...] = one_hot(((r2 & 7) == (c2 >> 5)) & ((c2 & 31).astype(F32) == row_here))
    diagonal = rows((64, 64)) == cols((64, 64))
    bias_half = jnp.sum(jnp.where(diagonal, 0.5 * bias_ref[...], 0.0), axis=1, keepdims=True)
    bias_col[...] = jnp.broadcast_to(bias_half, (64, 256))

    spread = one_hot((cols((8, 256)) >> 5) == rows((8, 256)))
    for tap in range(9):
        lanes[tap] = 0.5 * dot(weight_ref[tap], spread, ((0,), (0,)))
    row_lanes = (cols((8, 256)) & 31).astype(F32)

    @pl.loop(0, 16)
    def _(pair):
        start = pl.multiple_of(16 * pair, 16)
        delta = [row_lanes - row_col[pl.ds(start + 8 * k, 8)] for k in range(2)]
        for g in range(8):
            for dc in range(3):
                parts = []
                for k in range(2):
                    value = jnp.zeros((8, 256), F32)
                    for dr in range(3):
                        value = jnp.where(delta[k] == dr - 1.0, lanes[3 * dr + dc, 8 * g : 8 * g + 8], value)
                    parts.append(value)
                both = jnp.concatenate(parts, axis=0).astype(BF16)
                slot_band[g, pl.ds(start, 16), dc * 256 : (dc + 1) * 256] = both

    for copy in edge_copies:
        copy.wait()
    from_left = jnp.where(tile > 0, edge_in[0], nought[:, :128])
    from_right = jnp.where(tile < 7, edge_in[1], nought[:, :128])

    def fix(n, carry):
        old = wide[n, 0:256, 0:128]
        wide[n, 0:256, 0:128] = jnp.where(lane == 0, pltpu.roll(from_left, (128 - n) % 128, 1), old)
        old = wide[n, 512:768, 128:256]
        wide[n, 512:768, 128:256] = jnp.where(lane == 127, pltpu.roll(from_right, 111 - n, 1), old)
        return carry

    lax.fori_loop(0, 16, fix, 0, unroll=UNROLL)

    def slots(s):
        lo = 128 * s

        @pl.loop(0, 4, unroll=4)
        def _(pair):
            second = half_col[lo : lo + 128] > 0.5
            for f in range(2):
                parts = []
                for e in range(2):
                    g = 2 * pair + e
                    act = dot(slot_band[g, lo : lo + 128, :], wide[2 * g + f])
                    plain = dot(pick[lo : lo + 128, :], wide[2 * g + f, 256:512])
                    act = jnp.where(second, act[:, 128:], act[:, :128]).reshape(16, 8, 128)
                    plain = jnp.where(second, plain[:, 128:], plain[:, :128]).reshape(16, 8, 128)
                    act = act + bias_col[pl.ds(8 * g, 8), 0:128]
                    parts.append(plain + gated(act))
                joined = jnp.concatenate(parts, axis=1).astype(BF16)
                outgoing[16 * s : 16 * s + 16, f, pl.ds(16 * pair, 16), :] = joined

    copies = []

    def send(stage, source, target):
        for hop in HOPS:
            to = peer(hop)
            copy = pltpu.make_async_remote_copy(
                src_ref=source(to),
                dst_ref=target,
                send_sem=send_sems.at[stage],
                recv_sem=recv_sems.at[stage],
                device_id={"frame": to},
                device_id_type=MESH,
            )
            copy.start()

    def whole(stage, ref):
        return pltpu.make_async_remote_copy(
            src_ref=ref,
            dst_ref=ref,
            send_sem=send_sems.at[stage],
            recv_sem=recv_sems.at[stage],
            device_id={"frame": peer(HOPS[0])},
            device_id_type=MESH,
        )

    for s in range(2):
        slots(s)
        if s == 0:
            pl.semaphore_wait(row_sem, 3)
        else:
            whole(0, outgoing.at[pl.ds(0, 15)]).wait_send()
        send(s, lambda to, s=s: outgoing.at[16 * s + to], incoming.at[s, me])
        incoming[s, me] = outgoing[16 * s + me]

    offset = (cols((32, 256)) & 31) - rows((32, 256))

    @pl.loop(0, 8)
    def _(g):
        for dc in range(3):
            for o in range(8):
                value = jnp.zeros((32, 256), F32)
                for dr in range(3):
                    line = lanes[3 * dr + dc, pl.ds(8 * g + o, 1), :]
                    value = jnp.where(offset == dr - 1, line, value)
                band[g, o * 32 : (o + 1) * 32, dc * 256 : (dc + 1) * 256] = value.astype(BF16)

    expand = one_hot((cols((32, 256)) >> 3) == rows((32, 256)))
    row_lane = dot(jnp.broadcast_to(row_of, (8, 32)).astype(BF16), expand)[0:1]
    half_lane = dot(jnp.broadcast_to(half_of, (8, 32)).astype(BF16), expand)[0:1]
    live = (c2 >> 3) < count_ref[0]
    target = ((r2 >> 5) == (c2 & 7)) & ((r2 & 31).astype(F32) == row_lane) & live
    for h in range(2):
        chosen = jnp.where(target & (half_lane == float(h)), 1.0, 0.0)
        place[h * 256 : (h + 1) * 256, :] = chosen.astype(BF16)
        for s in range(2):
            found = jnp.sum(chosen[:, 128 * s : 128 * s + 128], axis=1, keepdims=True)
            covered[s, :, h * 128 : (h + 1) * 128] = jnp.broadcast_to(found, (256, 128))

    for layer in range(4):
        for j in range(3):
            line = 0.5 * depth_ref[j, layer : layer + 1, :]
            column = jnp.sum(jnp.where(diagonal, line, 0.0), axis=1, keepdims=True)
            taps[3 * layer + j] = jnp.broadcast_to(column, (64, 128))
    repeat = one_hot((rows((256, 64)) & 63) == cols((256, 64)))
    for layer in range(4):
        tall = dot(repeat, point_ref[layer]).astype(BF16)
        full = dot(tall, repeat, ((1,), (1,)))
        mix[layer] = jnp.where((r2 >> 6) == (c2 >> 6), full, 0.0).astype(BF16)

    @pl.loop(0, 8, unroll=2)
    def _(g):
        for f in range(2):
            act = dot(band[g], wide[2 * g + f])
            for o in range(8):
                half = act[o * 32 : (o + 1) * 32] + bias_col[pl.ds(8 * g + o, 1), :]
                value = cells[8 * g + o, f].astype(F32) + gated(half)
                out_ref[8 * g + o, f] = value.astype(BF16)

    def temporal(s):
        state[0:16] = jnp.zeros((16, 64, 128), F32)

        @pl.loop(0, 16, unroll=4)
        def _(p):
            state[pl.ds(16 + 2 * p, 2)] = incoming[s, p].astype(F32)

        for layer in range(4):
            d = 2**layer

            @pl.loop(0, 4, unroll=4)
            def _(i):
                base = 40 - 8 * i
                now = state[pl.ds(base, 8)]
                half = taps[3 * layer] * now
                half = half + taps[3 * layer + 1] * state[pl.ds(base - d, 8)]
                half = half + taps[3 * layer + 2] * state[pl.ds(base - 2 * d, 8)]
                squashed = gated(half).astype(BF16)
                pair = [squashed[0:4].reshape(256, 128), squashed[4:8].reshape(256, 128)]
                mixed = dot(mix[layer], jnp.concatenate(pair, axis=1))
                for h in range(2):
                    new = now[4 * h : 4 * h + 4] + mixed[:, 128 * h : 128 * h + 128].reshape(4, 64, 128)
                    if layer < 3:
                        state[pl.ds(base + 4 * h, 4)] = new
                    else:
                        answer[s, pl.ds(12 - 4 * i + 2 * h, 2)] = new.reshape(2, 2, 64, 128).astype(BF16)

    for s in range(2):
        whole(s, incoming.at[s, pl.ds(0, 15)]).wait_recv()
        temporal(s)
        send(2 + s, lambda to, s=s: answer.at[s, to], returned.at[16 * s + me])
        returned[16 * s + me] = answer[s, me]

    def merge(s):
        @pl.loop(0, 4, unroll=2)
        def _(pair):
            split = [returned[16 * s : 16 * s + 16, f, pl.ds(16 * pair, 16), :].astype(F32) for f in range(2)]
            for e in range(2):
                g = 2 * pair + e
                both = [part[:, 8 * e : 8 * e + 8].reshape(128, 128) for part in split]
                value = dot(place[:, 128 * s : 128 * s + 128], jnp.concatenate(both, axis=1).astype(BF16))
                for f in range(2):
                    for h in range(2):
                        span = slice(128 * h, 128 * h + 128)
                        new = value[256 * h : 256 * h + 256, 128 * f : 128 * f + 128]
                        old = out_ref[pl.ds(8 * g, 8), f, :, span].reshape(256, 128).astype(F32)
                        new = jnp.where(covered[s, :, span] > 0.5, new, old)
                        out_ref[pl.ds(8 * g, 8), f, :, span] = new.reshape(8, 32, 128).astype(BF16)

    for s in range(2):
        whole(2 + s, returned.at[pl.ds(0, 15)]).wait_recv()
        merge(s)

    for s in range(2):
        if s:
            whole(s, outgoing.at[pl.ds(0, 15)]).wait_send()
        whole(2 + s, answer.at[s, pl.ds(0, 15)]).wait_send()


def on_device(grid, conv_weight, conv_bias, depth_kernel, point_weight, occupied, counts):
    buffers = [
        ((64, 2, 32, 256), BF16),
        ((16, 768, 256), BF16),
        ((9, 64, 256), F32),
        ((8, 256, 768), BF16),
        ((8, 256, 768), BF16),
        ((256, 256), BF16),
        ((512, 256), BF16),
        ((2, 256, 256), F32),
        ((4, 256, 256), BF16),
        ((12, 64, 128), F32),
        ((64, 256), F32),
        ((256, 256), F32),
        ((256, 128), F32),
        ((256, 128), BF16),
        ((2, 256, 128), BF16),
        ((32, 2, 64, 128), BF16),
        ((2, 16, 2, 64, 128), BF16),
        ((48, 64, 128), F32),
        ((2, 16, 2, 64, 128), BF16),
        ((32, 2, 64, 128), BF16),
    ]
    return pl.pallas_call(
        kernel,
        out_shape=jax.ShapeDtypeStruct(grid.shape, grid.dtype),
        in_specs=[pl.BlockSpec(memory_space=pltpu.HBM)] * 7,
        out_specs=pl.BlockSpec(memory_space=pltpu.VMEM),
        scratch_shapes=[
            pltpu.VMEM((9, 8, 64), BF16),
            pltpu.VMEM((1, 64), F32),
            pltpu.VMEM((3, 4, 64), F32),
            pltpu.VMEM((4, 64, 64), BF16),
            pltpu.VMEM((1, 32), jnp.int32),
            pltpu.SMEM((1,), jnp.int32),
        ]
        + [pltpu.VMEM(shape, kind) for shape, kind in buffers]
        + [
            pltpu.SemaphoreType.DMA((11,)),
            pltpu.SemaphoreType.DMA((2,)),
            pltpu.SemaphoreType.DMA((2,)),
            pltpu.SemaphoreType.DMA((4,)),
            pltpu.SemaphoreType.DMA((4,)),
            pltpu.SemaphoreType.REGULAR,
        ],
        compiler_params=pltpu.CompilerParams(
            collective_id=0, has_side_effects=True, vmem_limit_bytes=36 * 1024 * 1024
        ),
        cost_estimate=pl.CostEstimate(flops=4_000_000_000, bytes_accessed=0, transcendentals=3 << 20),
    )(
        *(
            pltpu.with_memory_space_constraint(array, pltpu.HBM)
            for array in (
                grid,
                conv_weight.transpose(0, 2, 1),
                conv_bias.reshape(1, 64),
                depth_kernel.transpose(1, 0, 2),
                point_weight,
                occupied,
            )
        ),
        counts,
    )


def solution(mesh):
    placed = (P(None, "frame", None, "tile"), P(), P(), P(), P(), P("tile", None), P("tile"))
    return jax.shard_map(
        on_device,
        mesh=mesh,
        in_specs=placed,
        out_specs=P(None, "frame", None, "tile"),
        check_vma=False,
    )
```

```python
import functools

import jax
import jax.numpy as jnp
from jax import lax
from jax.experimental import pallas as pl
from jax.experimental.pallas import tpu as pltpu
from jax.sharding import PartitionSpec as P

MESH = pl.DeviceIdType.MESH
F32 = jnp.float32
BF16 = jnp.bfloat16
UNROLL = 16

HOPS = (
    (2, 2), (2, 1), (2, 3), (1, 2), (3, 2), (2, 0), (0, 2),
    (1, 1), (3, 3), (1, 3), (3, 1), (1, 0), (3, 0), (0, 1), (0, 3),
)


def rows(shape):
    return lax.broadcasted_iota(jnp.int32, shape, 0)


def cols(shape):
    return lax.broadcasted_iota(jnp.int32, shape, 1)


def one_hot(mask):
    return jnp.where(mask, 1.0, 0.0).astype(BF16)


def dot(lhs, rhs, contract=((1,), (0,))):
    return lax.dot_general(lhs, rhs, (contract, ((), ())), preferred_element_type=F32)


def gated(half):
    return half + half * jnp.tanh(half)


def kernel(
    grid_hbm, weight_hbm, bias_hbm, depth_hbm, point_hbm, occupied_hbm, count_hbm,
    out_ref, returned, place, covered_last,
    weight_ref, bias_ref, depth_ref, point_ref, occupied_ref, count_ref, cells, wide, lanes, band,
    slot_band, pick, covered, mix, taps, bias_col, row_col, half_col,
    edge_out, edge_in, outgoing, incoming, state, answer,
    load_sems, edge_send, edge_recv, send_sems, recv_sems, row_sem,
):
    me = lax.axis_index("frame")
    tile = lax.axis_index("tile")
    row, col = me // 4, me % 4
    right, left = {"tile": (tile + 1) % 8}, {"tile": (tile + 7) % 8}

    def peer(hop):
        return ((row + hop[0]) % 4) * 4 + (col + hop[1]) % 4

    barrier = pltpu.get_barrier_semaphore()
    for neighbour in (right, left):
        pl.semaphore_signal(barrier, inc=1, device_id=neighbour, device_id_type=MESH)
    for d in (2, 1, 3):
        for hop in ((d, 0), (0, d)):
            pl.semaphore_signal(barrier, inc=1, device_id={"frame": peer(hop)}, device_id_type=MESH)
    sources = (weight_hbm, bias_hbm, depth_hbm, point_hbm, occupied_hbm, count_hbm)
    targets = (weight_ref, bias_ref, depth_ref, point_ref, occupied_ref, count_ref)
    quarters = []
    for i in range(4):
        span = pl.ds(16 * i, 16)
        quarters.append(pltpu.make_async_copy(grid_hbm.at[span], cells.at[span], load_sems.at[7 + i]))
        quarters[i].start()
    loads = []
    for i, (source, target) in enumerate(zip(sources, targets)):
        loads.append(pltpu.make_async_copy(source, target, load_sems.at[i]))
        loads[i].start()

    lane, lane_wide = cols((32, 128)), cols((256, 256))
    nought = jnp.zeros((256, 256), BF16)

    def ends(n, edges):
        block = cells[pl.ds(8 * (n // 2), 8), n % 2]
        last, first = edges
        for i in range(8):
            last = jnp.where(lane == 16 * i + n, pltpu.roll(block[i, :, 128:], (16 * i + n + 1) % 128, 1), last)
            first = jnp.where(lane == 16 * i + n, pltpu.roll(block[i, :, :128], 16 * i + n, 1), first)
        return last, first

    edges = (nought[:32, :128], nought[:32, :128])
    for i in range(4):
        quarters[i].wait()
        edges = lax.fori_loop(4 * i, 4 * i + 4, ends, edges, unroll=4)
    edge_out[0], edge_out[1] = edges

    pl.semaphore_wait(barrier, 8)
    edge_copies = []
    for side, neighbour in enumerate((right, left)):
        copy = pltpu.make_async_remote_copy(
            src_ref=edge_out.at[side],
            dst_ref=edge_in.at[side],
            send_sem=edge_send.at[side],
            recv_sem=edge_recv.at[side],
            device_id=neighbour,
            device_id_type=MESH,
        )
        copy.start()
        edge_copies.append(copy)

    for d in (2, 1, 3):
        pl.semaphore_signal(row_sem, inc=1, device_id={"frame": peer((0, d))}, device_id_type=MESH)

    def shift(n, carry):
        block = cells[pl.ds(8 * (n // 2), 8), n % 2].reshape(256, 256)
        wide[n, 256:512] = block
        wide[n, 0:256] = jnp.where(lane_wide == 0, nought, pltpu.roll(block, 1, 1))
        wide[n, 512:768] = jnp.where(lane_wide == 255, nought, pltpu.roll(block, 255, 1))
        return carry

    lax.fori_loop(0, 16, shift, 0, unroll=UNROLL)

    for load in loads:
        load.wait()
    r2, c2 = rows((256, 256)), cols((256, 256))
    listed = occupied_ref[...]
    row_of = (listed >> 1).astype(F32)
    half_of = (listed & 1).astype(F32)
    own = cols((256, 32)) == (rows((256, 32)) >> 3)
    row_here = jnp.sum(jnp.where(own, row_of, 0.0), axis=1, keepdims=True)
    row_col[...] = jnp.broadcast_to(row_here, (256, 256))
    half_col[...] = jnp.broadcast_to(jnp.sum(jnp.where(own, half_of, 0.0), axis=1, keepdims=True), (256, 128))
    pick[...] = one_hot(((r2 & 7) == (c2 >> 5)) & ((c2 & 31).astype(F32) == row_here))
    diagonal = rows((64, 64)) == cols((64, 64))
    bias_half = jnp.sum(jnp.where(diagonal, 0.5 * bias_ref[...], 0.0), axis=1, keepdims=True)
    bias_col[...] = jnp.broadcast_to(bias_half, (64, 256))

    spread = one_hot((cols((8, 256)) >> 5) == rows((8, 256)))
    for tap in range(9):
        lanes[tap] = 0.5 * dot(weight_ref[tap], spread, ((0,), (0,)))
    row_lanes = (cols((8, 256)) & 31).astype(F32)

    def fill(s):
        @pl.loop(8 * s, 8 * s + 8)
        def _(pair):
            start = pl.multiple_of(16 * pair, 16)
            delta = [row_lanes - row_col[pl.ds(start + 8 * k, 8)] for k in range(2)]
            for g in range(8):
                for dc in range(3):
                    parts = []
                    for k in range(2):
                        value = jnp.zeros((8, 256), F32)
                        for dr in range(3):
                            value = jnp.where(delta[k] == dr - 1.0, lanes[3 * dr + dc, 8 * g : 8 * g + 8], value)
                        parts.append(value)
                    both = jnp.concatenate(parts, axis=0).astype(BF16)
                    slot_band[g, pl.ds(start, 16), dc * 256 : (dc + 1) * 256] = both

    fill(0)
    for copy in edge_copies:
        copy.wait()
    from_left = jnp.where(tile > 0, edge_in[0], nought[:32, :128])
    from_right = jnp.where(tile < 7, edge_in[1], nought[:32, :128])

    def fix(n, carry):
        for i in range(8):
            span = slice(32 * i, 32 * i + 32)
            edge = pltpu.roll(from_left, (128 - 16 * i - n) % 128, 1)
            wide[n, span, 0:128] = jnp.where(lane == 0, edge, wide[n, span, 0:128])
            span = slice(512 + 32 * i, 544 + 32 * i)
            edge = pltpu.roll(from_right, 127 - 16 * i - n, 1)
            wide[n, span, 128:256] = jnp.where(lane == 127, edge, wide[n, span, 128:256])
        return carry

    lax.fori_loop(0, 16, fix, 0, unroll=UNROLL)

    def slots(s):
        lo = 128 * s

        @pl.loop(0, 4, unroll=4)
        def _(pair):
            second = half_col[lo : lo + 128] > 0.5
            for f in range(2):
                parts = []
                for e in range(2):
                    g = 2 * pair + e
                    act = dot(slot_band[g, lo : lo + 128, :], wide[2 * g + f])
                    plain = dot(pick[lo : lo + 128, :], wide[2 * g + f, 256:512])
                    act = jnp.where(second, act[:, 128:], act[:, :128]).reshape(16, 8, 128)
                    plain = jnp.where(second, plain[:, 128:], plain[:, :128]).reshape(16, 8, 128)
                    act = act + bias_col[pl.ds(8 * g, 8), 0:128]
                    parts.append(plain + gated(act))
                joined = jnp.concatenate(parts, axis=1).astype(BF16)
                outgoing[16 * s : 16 * s + 16, f, pl.ds(16 * pair, 16), :] = joined

    copies = []

    def send(stage, source, target):
        for hop in HOPS:
            to = peer(hop)
            copy = pltpu.make_async_remote_copy(
                src_ref=source(to),
                dst_ref=target,
                send_sem=send_sems.at[stage],
                recv_sem=recv_sems.at[stage],
                device_id={"frame": to},
                device_id_type=MESH,
            )
            copy.start()

    def whole(stage, ref):
        return pltpu.make_async_remote_copy(
            src_ref=ref,
            dst_ref=ref,
            send_sem=send_sems.at[stage],
            recv_sem=recv_sems.at[stage],
            device_id={"frame": peer(HOPS[0])},
            device_id_type=MESH,
        )

    for s in range(2):
        if s == 1:
            fill(1)
        slots(s)
        if s == 0:
            pl.semaphore_wait(row_sem, 3)
        else:
            whole(0, outgoing.at[pl.ds(0, 15)]).wait_send()
        send(s, lambda to, s=s: outgoing.at[16 * s + to], incoming.at[s, me])
        incoming[s, me] = outgoing[16 * s + me]

    offset = (cols((32, 256)) & 31) - rows((32, 256))

    @pl.loop(0, 8)
    def _(g):
        for dc in range(3):
            for o in range(8):
                value = jnp.zeros((32, 256), F32)
                for dr in range(3):
                    line = lanes[3 * dr + dc, pl.ds(8 * g + o, 1), :]
                    value = jnp.where(offset == dr - 1, line, value)
                band[g, o * 32 : (o + 1) * 32, dc * 256 : (dc + 1) * 256] = value.astype(BF16)

    expand = one_hot((cols((32, 256)) >> 3) == rows((32, 256)))
    row_lane = dot(jnp.broadcast_to(row_of, (8, 32)).astype(BF16), expand)[0:1]
    half_lane = dot(jnp.broadcast_to(half_of, (8, 32)).astype(BF16), expand)[0:1]
    live = (c2 >> 3) < count_ref[0]
    target = ((r2 >> 5) == (c2 & 7)) & ((r2 & 31).astype(F32) == row_lane) & live
    for h in range(2):
        chosen = jnp.where(target & (half_lane == float(h)), 1.0, 0.0)
        place[h * 256 : (h + 1) * 256, :] = chosen.astype(BF16)
        for s in range(2):
            found = jnp.sum(chosen[:, 128 * s : 128 * s + 128], axis=1, keepdims=True)
            cover = covered if s == 0 else covered_last
            cover[:, h * 128 : (h + 1) * 128] = jnp.broadcast_to(found, (256, 128))

    for layer in range(4):
        for j in range(3):
            line = 0.5 * depth_ref[j, layer : layer + 1, :]
            column = jnp.sum(jnp.where(diagonal, line, 0.0), axis=1, keepdims=True)
            taps[3 * layer + j] = jnp.broadcast_to(column, (64, 128))
    repeat = one_hot((rows((256, 64)) & 63) == cols((256, 64)))
    for layer in range(4):
        tall = dot(repeat, point_ref[layer]).astype(BF16)
        full = dot(tall, repeat, ((1,), (1,)))
        mix[layer] = jnp.where((r2 >> 6) == (c2 >> 6), full, 0.0).astype(BF16)

    @pl.loop(0, 8, unroll=2)
    def _(g):
        for f in range(2):
            act = dot(band[g], wide[2 * g + f])
            for o in range(8):
                half = act[o * 32 : (o + 1) * 32] + bias_col[pl.ds(8 * g + o, 1), :]
                value = cells[8 * g + o, f].astype(F32) + gated(half)
                out_ref[8 * g + o, f] = value.astype(BF16)

    def temporal(s):
        state[0:16] = jnp.zeros((16, 64, 128), F32)

        @pl.loop(0, 16, unroll=4)
        def _(p):
            state[pl.ds(16 + 2 * p, 2)] = incoming[s, p].astype(F32)

        for layer in range(4):
            d = 2**layer

            @pl.loop(0, 4, unroll=4)
            def _(i):
                base = 40 - 8 * i
                now = state[pl.ds(base, 8)]
                half = taps[3 * layer] * now
                half = half + taps[3 * layer + 1] * state[pl.ds(base - d, 8)]
                half = half + taps[3 * layer + 2] * state[pl.ds(base - 2 * d, 8)]
                squashed = gated(half).astype(BF16)
                pair = [squashed[0:4].reshape(256, 128), squashed[4:8].reshape(256, 128)]
                mixed = dot(mix[layer], jnp.concatenate(pair, axis=1))
                for h in range(2):
                    new = now[4 * h : 4 * h + 4] + mixed[:, 128 * h : 128 * h + 128].reshape(4, 64, 128)
                    if layer < 3:
                        state[pl.ds(base + 4 * h, 4)] = new
                    else:
                        answer[s, pl.ds(12 - 4 * i + 2 * h, 2)] = new.reshape(2, 2, 64, 128).astype(BF16)

    for s in range(2):
        whole(s, incoming.at[s, pl.ds(0, 15)]).wait_recv()
        temporal(s)
        send(2 + s, lambda to, s=s: answer.at[s, to], returned.at[16 * s + me])
        returned[16 * s + me] = answer[s, me]

    for s in range(2):
        whole(2 + s, returned.at[pl.ds(0, 15)]).wait_recv()
        if s == 0:
            pl.loop(0, 4, unroll=2)(functools.partial(merge, s, out_ref, out_ref, returned, place, covered))

    for s in range(2):
        if s:
            whole(s, outgoing.at[pl.ds(0, 15)]).wait_send()
        whole(2 + s, answer.at[s, pl.ds(0, 15)]).wait_send()


def merge(s, old_ref, new_ref, returned, place, covered, pair):
    split = [returned[16 * s : 16 * s + 16, f, pl.ds(16 * pair, 16), :].astype(F32) for f in range(2)]
    for e in range(2):
        g = 2 * pair + e
        both = [part[:, 8 * e : 8 * e + 8].reshape(128, 128) for part in split]
        value = dot(place[:, 128 * s : 128 * s + 128], jnp.concatenate(both, axis=1).astype(BF16))
        for f in range(2):
            for h in range(2):
                span = slice(128 * h, 128 * h + 128)
                new = value[256 * h : 256 * h + 256, 128 * f : 128 * f + 128]
                old = old_ref[pl.ds(8 * g, 8), f, :, span].reshape(256, 128).astype(F32)
                new = jnp.where(covered[:, span] > 0.5, new, old)
                new_ref[pl.ds(8 * g, 8), f, :, span] = new.reshape(8, 32, 128).astype(BF16)


def finish(old_ref, returned, place, covered, out_hbm, out, sems):
    copies = []
    for pair in range(4):
        merge(1, old_ref, out, returned, place, covered, pair)
        span = pl.ds(16 * pair, 16)
        copies.append(pltpu.make_async_copy(out.at[span], out_hbm.at[span], sems.at[pair]))
        copies[pair].start()
    for copy in copies:
        copy.wait()


def on_device(grid, conv_weight, conv_bias, depth_kernel, point_weight, occupied, counts):
    buffers = [
        ((64, 2, 32, 256), BF16),
        ((16, 768, 256), BF16),
        ((9, 64, 256), F32),
        ((8, 256, 768), BF16),
        ((8, 256, 768), BF16),
        ((256, 256), BF16),
        ((256, 256), F32),
        ((4, 256, 256), BF16),
        ((12, 64, 128), F32),
        ((64, 256), F32),
        ((256, 256), F32),
        ((256, 128), F32),
        ((2, 32, 128), BF16),
        ((2, 32, 128), BF16),
        ((32, 2, 64, 128), BF16),
        ((2, 16, 2, 64, 128), BF16),
        ((48, 64, 128), F32),
        ((2, 16, 2, 64, 128), BF16),
    ]
    kinds = [(grid.shape, BF16), ((32, 2, 64, 128), BF16), ((512, 256), BF16), ((256, 256), F32)]
    vmem = pl.BlockSpec(memory_space=pltpu.VMEM)
    parts = pl.pallas_call(
        kernel,
        out_shape=[jax.ShapeDtypeStruct(shape, kind) for shape, kind in kinds],
        in_specs=[pl.BlockSpec(memory_space=pltpu.HBM)] * 7,
        out_specs=[vmem] * 4,
        scratch_shapes=[
            pltpu.VMEM((9, 8, 64), BF16),
            pltpu.VMEM((1, 64), F32),
            pltpu.VMEM((3, 4, 64), F32),
            pltpu.VMEM((4, 64, 64), BF16),
            pltpu.VMEM((1, 32), jnp.int32),
            pltpu.SMEM((1,), jnp.int32),
        ]
        + [pltpu.VMEM(shape, kind) for shape, kind in buffers]
        + [
            pltpu.SemaphoreType.DMA((11,)),
            pltpu.SemaphoreType.DMA((2,)),
            pltpu.SemaphoreType.DMA((2,)),
            pltpu.SemaphoreType.DMA((4,)),
            pltpu.SemaphoreType.DMA((4,)),
            pltpu.SemaphoreType.REGULAR,
        ],
        compiler_params=pltpu.CompilerParams(
            collective_id=0, has_side_effects=True, vmem_limit_bytes=36 * 1024 * 1024
        ),
        cost_estimate=pl.CostEstimate(flops=4_000_000_000, bytes_accessed=0, transcendentals=3 << 20),
    )(
        *(
            pltpu.with_memory_space_constraint(array, pltpu.HBM)
            for array in (
                grid,
                conv_weight.transpose(0, 2, 1),
                conv_bias.reshape(1, 64),
                depth_kernel.transpose(1, 0, 2),
                point_weight,
                occupied,
            )
        ),
        counts,
    )
    return pl.pallas_call(
        finish,
        out_shape=jax.ShapeDtypeStruct(grid.shape, grid.dtype),
        in_specs=[vmem] * 4,
        out_specs=pl.BlockSpec(memory_space=pl.ANY),
        scratch_shapes=[pltpu.VMEM(grid.shape, BF16), pltpu.SemaphoreType.DMA((4,))],
        compiler_params=pltpu.CompilerParams(vmem_limit_bytes=36 * 1024 * 1024),
    )(*parts)


def solution(mesh):
    placed = (P(None, "frame", None, "tile"), P(), P(), P(), P(), P("tile", None), P("tile"))
    return jax.shard_map(
        on_device,
        mesh=mesh,
        in_specs=placed,
        out_specs=P(None, "frame", None, "tile"),
        check_vma=False,
    )
```

```python
import functools

import jax
import jax.numpy as jnp
from jax import lax
from jax.experimental import pallas as pl
from jax.experimental.pallas import tpu as pltpu
from jax.sharding import PartitionSpec as P

MESH = pl.DeviceIdType.MESH
F32 = jnp.float32
BF16 = jnp.bfloat16
UNROLL = 16

HOPS = (
    (2, 2), (2, 1), (2, 3), (1, 2), (3, 2), (2, 0), (0, 2),
    (1, 1), (3, 3), (1, 3), (3, 1), (1, 0), (3, 0), (0, 1), (0, 3),
)


def rows(shape):
    return lax.broadcasted_iota(jnp.int32, shape, 0)


def cols(shape):
    return lax.broadcasted_iota(jnp.int32, shape, 1)


def one_hot(mask):
    return jnp.where(mask, 1.0, 0.0).astype(BF16)


def dot(lhs, rhs, contract=((1,), (0,))):
    return lax.dot_general(lhs, rhs, (contract, ((), ())), preferred_element_type=F32)


def gated(half):
    return half + half * jnp.tanh(half)


def kernel(
    grid_hbm, weight_hbm, bias_hbm, depth_hbm, point_hbm, occupied_hbm, count_hbm,
    out_ref, returned, place, covered_last,
    weight_ref, bias_ref, depth_ref, point_ref, occupied_ref, count_ref, cells, wide, lanes, band,
    slot_band, pick, covered, mix, taps, bias_col, row_col, half_col,
    edge_out, edge_in, outgoing, incoming, state, answer,
    load_sems, edge_send, edge_recv, send_sems, recv_sems, row_sem,
):
    me = lax.axis_index("frame")
    tile = lax.axis_index("tile")
    row, col = me // 4, me % 4
    right, left = {"tile": (tile + 1) % 8}, {"tile": (tile + 7) % 8}

    def peer(hop):
        return ((row + hop[0]) % 4) * 4 + (col + hop[1]) % 4

    barrier = pltpu.get_barrier_semaphore()
    for neighbour in (right, left):
        pl.semaphore_signal(barrier, inc=1, device_id=neighbour, device_id_type=MESH)
    for d in (2, 1, 3):
        for hop in ((d, 0), (0, d)):
            pl.semaphore_signal(barrier, inc=1, device_id={"frame": peer(hop)}, device_id_type=MESH)
    sources = (weight_hbm, bias_hbm, depth_hbm, point_hbm, occupied_hbm, count_hbm)
    targets = (weight_ref, bias_ref, depth_ref, point_ref, occupied_ref, count_ref)
    quarters = []
    for i in range(4):
        span = pl.ds(16 * i, 16)
        quarters.append(pltpu.make_async_copy(grid_hbm.at[span], cells.at[span], load_sems.at[7 + i]))
        quarters[i].start()
    loads = []
    for i, (source, target) in enumerate(zip(sources, targets)):
        loads.append(pltpu.make_async_copy(source, target, load_sems.at[i]))
        loads[i].start()

    lane, lane_wide = cols((32, 128)), cols((256, 256))
    nought = jnp.zeros((256, 256), BF16)

    def ends(n, edges):
        block = cells[pl.ds(8 * (n // 2), 8), n % 2]
        last, first = edges
        for i in range(8):
            last = jnp.where(lane == 16 * i + n, pltpu.roll(block[i, :, 128:], (16 * i + n + 1) % 128, 1), last)
            first = jnp.where(lane == 16 * i + n, pltpu.roll(block[i, :, :128], 16 * i + n, 1), first)
        return last, first

    edges = (nought[:32, :128], nought[:32, :128])
    for i in range(4):
        quarters[i].wait()
        edges = lax.fori_loop(4 * i, 4 * i + 4, ends, edges, unroll=4)
    edge_out[0], edge_out[1] = edges

    pl.semaphore_wait(barrier, 8)
    edge_copies = []
    for side, neighbour in enumerate((right, left)):
        copy = pltpu.make_async_remote_copy(
            src_ref=edge_out.at[side],
            dst_ref=edge_in.at[side],
            send_sem=edge_send.at[side],
            recv_sem=edge_recv.at[side],
            device_id=neighbour,
            device_id_type=MESH,
        )
        copy.start()
        edge_copies.append(copy)

    for d in (2, 1, 3):
        pl.semaphore_signal(row_sem, inc=1, device_id={"frame": peer((0, d))}, device_id_type=MESH)

    def shift(n, carry):
        block = cells[pl.ds(8 * (n // 2), 8), n % 2].reshape(256, 256)
        wide[n, 256:512] = block
        wide[n, 0:256] = jnp.where(lane_wide == 0, nought, pltpu.roll(block, 1, 1))
        wide[n, 512:768] = jnp.where(lane_wide == 255, nought, pltpu.roll(block, 255, 1))
        return carry

    lax.fori_loop(0, 16, shift, 0, unroll=UNROLL)

    for load in loads:
        load.wait()
    r2, c2 = rows((256, 256)), cols((256, 256))
    listed = occupied_ref[...]
    row_of = (listed >> 1).astype(F32)
    half_of = (listed & 1).astype(F32)
    own = cols((256, 32)) == (rows((256, 32)) >> 3)
    row_here = jnp.sum(jnp.where(own, row_of, 0.0), axis=1, keepdims=True)
    row_col[...] = jnp.broadcast_to(row_here, (256, 256))
    half_col[...] = jnp.broadcast_to(jnp.sum(jnp.where(own, half_of, 0.0), axis=1, keepdims=True), (256, 128))
    pick[...] = one_hot(((r2 & 7) == (c2 >> 5)) & ((c2 & 31).astype(F32) == row_here))
    diagonal = rows((64, 64)) == cols((64, 64))
    bias_half = jnp.sum(jnp.where(diagonal, 0.5 * bias_ref[...], 0.0), axis=1, keepdims=True)
    bias_col[...] = jnp.broadcast_to(bias_half, (64, 256))

    spread = one_hot((cols((8, 256)) >> 5) == rows((8, 256)))
    for tap in range(9):
        lanes[tap] = 0.5 * dot(weight_ref[tap], spread, ((0,), (0,)))
    row_lanes = (cols((8, 256)) & 31).astype(F32)

    def fill(s):
        @pl.loop(8 * s, 8 * s + 8)
        def _(pair):
            start = pl.multiple_of(16 * pair, 16)
            delta = [row_lanes - row_col[pl.ds(start + 8 * k, 8)] for k in range(2)]
            for g in range(8):
                for dc in range(3):
                    parts = []
                    for k in range(2):
                        value = jnp.zeros((8, 256), F32)
                        for dr in range(3):
                            value = jnp.where(delta[k] == dr - 1.0, lanes[3 * dr + dc, 8 * g : 8 * g + 8], value)
                        parts.append(value)
                    both = jnp.concatenate(parts, axis=0).astype(BF16)
                    slot_band[g, pl.ds(start, 16), dc * 256 : (dc + 1) * 256] = both

    fill(0)
    for copy in edge_copies:
        copy.wait()
    from_left = jnp.where(tile > 0, edge_in[0], nought[:32, :128])
    from_right = jnp.where(tile < 7, edge_in[1], nought[:32, :128])

    def fix(g, f):
        n = 2 * g + f
        for i in range(8):
            span = slice(32 * i, 32 * i + 32)
            edge = pltpu.roll(from_left, (128 - 16 * i - n) % 128, 1)
            wide[n, span, 0:128] = jnp.where(lane == 0, edge, wide[n, span, 0:128])
            span = slice(512 + 32 * i, 544 + 32 * i)
            edge = pltpu.roll(from_right, 127 - 16 * i - n, 1)
            wide[n, span, 128:256] = jnp.where(lane == 127, edge, wide[n, span, 128:256])
        return f


    def slots(s, frames=(0, 1)):
        lo = 128 * s

        @pl.loop(0, 4, unroll=4)
        def _(pair):
            second = half_col[lo : lo + 128] > 0.5
            for f in frames:
                parts = []
                for e in range(2):
                    g = 2 * pair + e
                    act = dot(slot_band[g, lo : lo + 128, :], wide[2 * g + f])
                    plain = dot(pick[lo : lo + 128, :], wide[2 * g + f, 256:512])
                    act = jnp.where(second, act[:, 128:], act[:, :128]).reshape(16, 8, 128)
                    plain = jnp.where(second, plain[:, 128:], plain[:, :128]).reshape(16, 8, 128)
                    act = act + bias_col[pl.ds(8 * g, 8), 0:128]
                    parts.append(plain + gated(act))
                joined = jnp.concatenate(parts, axis=1).astype(BF16)
                outgoing[16 * s : 16 * s + 16, f, pl.ds(16 * pair, 16), :] = joined

    copies = []

    def send(stage, source, target):
        for hop in HOPS:
            to = peer(hop)
            copy = pltpu.make_async_remote_copy(
                src_ref=source(to),
                dst_ref=target,
                send_sem=send_sems.at[stage],
                recv_sem=recv_sems.at[stage],
                device_id={"frame": to},
                device_id_type=MESH,
            )
            copy.start()

    def whole(stage, ref):
        return pltpu.make_async_remote_copy(
            src_ref=ref,
            dst_ref=ref,
            send_sem=send_sems.at[stage],
            recv_sem=recv_sems.at[stage],
            device_id={"frame": peer(HOPS[0])},
            device_id_type=MESH,
        )

    for s in range(2):
        if s == 1:
            fill(1)
        if s == 0:
            for f in range(2):
                lax.fori_loop(0, 8, fix, f, unroll=8)
                slots(0, (f,))
                if f == 0:
                    pl.semaphore_wait(row_sem, 3)
                send(0, lambda to, f=f: outgoing.at[to, f], incoming.at[0, me, f])
        else:
            slots(1)
            whole(0, outgoing.at[pl.ds(0, 15)]).wait_send()
            send(1, lambda to: outgoing.at[16 + to], incoming.at[1, me])
        incoming[s, me] = outgoing[16 * s + me]

    offset = (cols((32, 256)) & 31) - rows((32, 256))

    @pl.loop(0, 8)
    def _(g):
        for dc in range(3):
            for o in range(8):
                value = jnp.zeros((32, 256), F32)
                for dr in range(3):
                    line = lanes[3 * dr + dc, pl.ds(8 * g + o, 1), :]
                    value = jnp.where(offset == dr - 1, line, value)
                band[g, o * 32 : (o + 1) * 32, dc * 256 : (dc + 1) * 256] = value.astype(BF16)

    expand = one_hot((cols((32, 256)) >> 3) == rows((32, 256)))
    row_lane = dot(jnp.broadcast_to(row_of, (8, 32)).astype(BF16), expand)[0:1]
    half_lane = dot(jnp.broadcast_to(half_of, (8, 32)).astype(BF16), expand)[0:1]
    live = (c2 >> 3) < count_ref[0]
    target = ((r2 >> 5) == (c2 & 7)) & ((r2 & 31).astype(F32) == row_lane) & live
    for h in range(2):
        chosen = jnp.where(target & (half_lane == float(h)), 1.0, 0.0)
        place[h * 256 : (h + 1) * 256, :] = chosen.astype(BF16)
        for s in range(2):
            found = jnp.sum(chosen[:, 128 * s : 128 * s + 128], axis=1, keepdims=True)
            cover = covered if s == 0 else covered_last
            cover[:, h * 128 : (h + 1) * 128] = jnp.broadcast_to(found, (256, 128))

    for layer in range(4):
        for j in range(3):
            line = 0.5 * depth_ref[j, layer : layer + 1, :]
            column = jnp.sum(jnp.where(diagonal, line, 0.0), axis=1, keepdims=True)
            taps[3 * layer + j] = jnp.broadcast_to(column, (64, 128))
    repeat = one_hot((rows((256, 64)) & 63) == cols((256, 64)))
    for layer in range(4):
        tall = dot(repeat, point_ref[layer]).astype(BF16)
        full = dot(tall, repeat, ((1,), (1,)))
        mix[layer] = jnp.where((r2 >> 6) == (c2 >> 6), full, 0.0).astype(BF16)

    @pl.loop(0, 8, unroll=2)
    def _(g):
        for f in range(2):
            act = dot(band[g], wide[2 * g + f])
            for o in range(8):
                half = act[o * 32 : (o + 1) * 32] + bias_col[pl.ds(8 * g + o, 1), :]
                value = cells[8 * g + o, f].astype(F32) + gated(half)
                out_ref[8 * g + o, f] = value.astype(BF16)

    def temporal(s):
        state[0:16] = jnp.zeros((16, 64, 128), F32)

        @pl.loop(0, 16, unroll=4)
        def _(p):
            state[pl.ds(16 + 2 * p, 2)] = incoming[s, p].astype(F32)

        for layer in range(4):
            d = 2**layer

            @pl.loop(0, 4, unroll=4)
            def _(i):
                base = 40 - 8 * i
                now = state[pl.ds(base, 8)]
                half = taps[3 * layer] * now
                half = half + taps[3 * layer + 1] * state[pl.ds(base - d, 8)]
                half = half + taps[3 * layer + 2] * state[pl.ds(base - 2 * d, 8)]
                squashed = gated(half).astype(BF16)
                pair = [squashed[0:4].reshape(256, 128), squashed[4:8].reshape(256, 128)]
                mixed = dot(mix[layer], jnp.concatenate(pair, axis=1))
                for h in range(2):
                    new = now[4 * h : 4 * h + 4] + mixed[:, 128 * h : 128 * h + 128].reshape(4, 64, 128)
                    if layer < 3:
                        state[pl.ds(base + 4 * h, 4)] = new
                    else:
                        answer[s, pl.ds(12 - 4 * i + 2 * h, 2)] = new.reshape(2, 2, 64, 128).astype(BF16)

    for s in range(2):
        whole(s, incoming.at[s, pl.ds(0, 15)]).wait_recv()
        temporal(s)
        send(2 + s, lambda to, s=s: answer.at[s, to], returned.at[16 * s + me])
        returned[16 * s + me] = answer[s, me]

    for s in range(2):
        whole(2 + s, returned.at[pl.ds(0, 15)]).wait_recv()
        if s == 0:
            pl.loop(0, 4, unroll=2)(functools.partial(merge, s, out_ref, out_ref, returned, place, covered))

    for s in range(2):
        if s:
            whole(s, outgoing.at[pl.ds(0, 15)]).wait_send()
        whole(2 + s, answer.at[s, pl.ds(0, 15)]).wait_send()


def merge(s, old_ref, new_ref, returned, place, covered, pair):
    split = [returned[16 * s : 16 * s + 16, f, pl.ds(16 * pair, 16), :].astype(F32) for f in range(2)]
    for e in range(2):
        g = 2 * pair + e
        both = [part[:, 8 * e : 8 * e + 8].reshape(128, 128) for part in split]
        value = dot(place[:, 128 * s : 128 * s + 128], jnp.concatenate(both, axis=1).astype(BF16))
        for f in range(2):
            for h in range(2):
                span = slice(128 * h, 128 * h + 128)
                new = value[256 * h : 256 * h + 256, 128 * f : 128 * f + 128]
                old = old_ref[pl.ds(8 * g, 8), f, :, span].reshape(256, 128).astype(F32)
                new = jnp.where(covered[:, span] > 0.5, new, old)
                new_ref[pl.ds(8 * g, 8), f, :, span] = new.reshape(8, 32, 128).astype(BF16)


def finish(old_ref, returned, place, covered, out_hbm, out, sems):
    copies = []
    for pair in range(4):
        merge(1, old_ref, out, returned, place, covered, pair)
        span = pl.ds(16 * pair, 16)
        copies.append(pltpu.make_async_copy(out.at[span], out_hbm.at[span], sems.at[pair]))
        copies[pair].start()
    for copy in copies:
        copy.wait()


def on_device(grid, conv_weight, conv_bias, depth_kernel, point_weight, occupied, counts):
    buffers = [
        ((64, 2, 32, 256), BF16),
        ((16, 768, 256), BF16),
        ((9, 64, 256), F32),
        ((8, 256, 768), BF16),
        ((8, 256, 768), BF16),
        ((256, 256), BF16),
        ((256, 256), F32),
        ((4, 256, 256), BF16),
        ((12, 64, 128), F32),
        ((64, 256), F32),
        ((256, 256), F32),
        ((256, 128), F32),
        ((2, 32, 128), BF16),
        ((2, 32, 128), BF16),
        ((32, 2, 64, 128), BF16),
        ((2, 16, 2, 64, 128), BF16),
        ((48, 64, 128), F32),
        ((2, 16, 2, 64, 128), BF16),
    ]
    kinds = [(grid.shape, BF16), ((32, 2, 64, 128), BF16), ((512, 256), BF16), ((256, 256), F32)]
    vmem = pl.BlockSpec(memory_space=pltpu.VMEM)
    parts = pl.pallas_call(
        kernel,
        out_shape=[jax.ShapeDtypeStruct(shape, kind) for shape, kind in kinds],
        in_specs=[pl.BlockSpec(memory_space=pltpu.HBM)] * 7,
        out_specs=[vmem] * 4,
        scratch_shapes=[
            pltpu.VMEM((9, 8, 64), BF16),
            pltpu.VMEM((1, 64), F32),
            pltpu.VMEM((3, 4, 64), F32),
            pltpu.VMEM((4, 64, 64), BF16),
            pltpu.VMEM((1, 32), jnp.int32),
            pltpu.SMEM((1,), jnp.int32),
        ]
        + [pltpu.VMEM(shape, kind) for shape, kind in buffers]
        + [
            pltpu.SemaphoreType.DMA((11,)),
            pltpu.SemaphoreType.DMA((2,)),
            pltpu.SemaphoreType.DMA((2,)),
            pltpu.SemaphoreType.DMA((4,)),
            pltpu.SemaphoreType.DMA((4,)),
            pltpu.SemaphoreType.REGULAR,
        ],
        compiler_params=pltpu.CompilerParams(
            collective_id=0, has_side_effects=True, vmem_limit_bytes=36 * 1024 * 1024
        ),
        cost_estimate=pl.CostEstimate(flops=4_000_000_000, bytes_accessed=0, transcendentals=3 << 20),
    )(
        *(
            pltpu.with_memory_space_constraint(array, pltpu.HBM)
            for array in (
                grid,
                conv_weight.transpose(0, 2, 1),
                conv_bias.reshape(1, 64),
                depth_kernel.transpose(1, 0, 2),
                point_weight,
                occupied,
            )
        ),
        counts,
    )
    return pl.pallas_call(
        finish,
        out_shape=jax.ShapeDtypeStruct(grid.shape, grid.dtype),
        in_specs=[vmem] * 4,
        out_specs=pl.BlockSpec(memory_space=pl.ANY),
        scratch_shapes=[pltpu.VMEM(grid.shape, BF16), pltpu.SemaphoreType.DMA((4,))],
        compiler_params=pltpu.CompilerParams(vmem_limit_bytes=36 * 1024 * 1024),
    )(*parts)


def solution(mesh):
    placed = (P(None, "frame", None, "tile"), P(), P(), P(), P(), P("tile", None), P("tile"))
    return jax.shard_map(
        on_device,
        mesh=mesh,
        in_specs=placed,
        out_specs=P(None, "frame", None, "tile"),
        check_vma=False,
    )
```

```python
import functools

import jax
import jax.numpy as jnp
from jax import lax
from jax.experimental import pallas as pl
from jax.experimental.pallas import tpu as pltpu
from jax.sharding import PartitionSpec as P

MESH = pl.DeviceIdType.MESH
F32 = jnp.float32
BF16 = jnp.bfloat16
UNROLL = 16

HOPS = (
    (2, 2), (2, 1), (2, 3), (1, 2), (3, 2), (2, 0), (0, 2),
    (1, 1), (3, 3), (1, 3), (3, 1), (1, 0), (3, 0), (0, 1), (0, 3),
)


def rows(shape):
    return lax.broadcasted_iota(jnp.int32, shape, 0)


def cols(shape):
    return lax.broadcasted_iota(jnp.int32, shape, 1)


def one_hot(mask):
    return jnp.where(mask, 1.0, 0.0).astype(BF16)


def dot(lhs, rhs, contract=((1,), (0,))):
    return lax.dot_general(lhs, rhs, (contract, ((), ())), preferred_element_type=F32)


def gated(half):
    return half + half * jnp.tanh(half)


def kernel(
    grid_hbm, weight_hbm, bias_hbm, depth_hbm, point_hbm, occupied_hbm, count_hbm,
    out_ref, returned, place, covered_last,
    weight_ref, bias_ref, depth_ref, point_ref, occupied_ref, count_ref, cells, wide, lanes, band,
    slot_band, pick, covered, mix, taps, bias_col, row_col, half_col,
    edge_out, edge_in, outgoing, incoming, state, answer,
    load_sems, edge_send, edge_recv, send_sems, recv_sems, row_sem,
):
    me = lax.axis_index("frame")
    tile = lax.axis_index("tile")
    row, col = me // 4, me % 4
    right, left = {"tile": (tile + 1) % 8}, {"tile": (tile + 7) % 8}

    def peer(hop):
        return ((row + hop[0]) % 4) * 4 + (col + hop[1]) % 4

    barrier = pltpu.get_barrier_semaphore()
    for neighbour in (right, left):
        pl.semaphore_signal(barrier, inc=1, device_id=neighbour, device_id_type=MESH)
    for d in (2, 1, 3):
        for hop in ((d, 0), (0, d)):
            pl.semaphore_signal(barrier, inc=1, device_id={"frame": peer(hop)}, device_id_type=MESH)
    sources = (weight_hbm, bias_hbm, depth_hbm, point_hbm, occupied_hbm, count_hbm)
    targets = (weight_ref, bias_ref, depth_ref, point_ref, occupied_ref, count_ref)
    quarters = []
    for i in range(4):
        span = pl.ds(16 * i, 16)
        quarters.append(pltpu.make_async_copy(grid_hbm.at[span], cells.at[span], load_sems.at[7 + i]))
        quarters[i].start()
    loads = []
    for i, (source, target) in enumerate(zip(sources, targets)):
        loads.append(pltpu.make_async_copy(source, target, load_sems.at[i]))
        loads[i].start()

    lane, lane_wide = cols((32, 128)), cols((256, 256))
    nought = jnp.zeros((256, 256), BF16)

    def ends(n, edges):
        block = cells[pl.ds(8 * (n // 2), 8), n % 2]
        last, first = edges
        for i in range(8):
            last = jnp.where(lane == 16 * i + n, pltpu.roll(block[i, :, 128:], (16 * i + n + 1) % 128, 1), last)
            first = jnp.where(lane == 16 * i + n, pltpu.roll(block[i, :, :128], 16 * i + n, 1), first)
        return last, first

    edges = (nought[:32, :128], nought[:32, :128])
    for i in range(4):
        quarters[i].wait()
        edges = lax.fori_loop(4 * i, 4 * i + 4, ends, edges, unroll=4)
    edge_out[0], edge_out[1] = edges

    pl.semaphore_wait(barrier, 8)
    edge_copies = []
    for side, neighbour in enumerate((right, left)):
        copy = pltpu.make_async_remote_copy(
            src_ref=edge_out.at[side],
            dst_ref=edge_in.at[side],
            send_sem=edge_send.at[side],
            recv_sem=edge_recv.at[side],
            device_id=neighbour,
            device_id_type=MESH,
        )
        copy.start()
        edge_copies.append(copy)

    for d in (2, 1, 3):
        pl.semaphore_signal(row_sem, inc=1, device_id={"frame": peer((0, d))}, device_id_type=MESH)

    def shift(n, carry):
        block = cells[pl.ds(8 * (n // 2), 8), n % 2].reshape(256, 256)
        wide[n, 256:512] = block
        wide[n, 0:256] = jnp.where(lane_wide == 0, nought, pltpu.roll(block, 1, 1))
        wide[n, 512:768] = jnp.where(lane_wide == 255, nought, pltpu.roll(block, 255, 1))
        return carry

    lax.fori_loop(0, 16, shift, 0, unroll=UNROLL)

    for load in loads:
        load.wait()
    r2, c2 = rows((256, 256)), cols((256, 256))
    listed = occupied_ref[...]
    row_of = (listed >> 1).astype(F32)
    half_of = (listed & 1).astype(F32)
    own = cols((256, 32)) == (rows((256, 32)) >> 3)
    row_here = jnp.sum(jnp.where(own, row_of, 0.0), axis=1, keepdims=True)
    row_col[...] = jnp.broadcast_to(row_here, (256, 256))
    half_col[...] = jnp.broadcast_to(jnp.sum(jnp.where(own, half_of, 0.0), axis=1, keepdims=True), (256, 128))
    pick[...] = one_hot(((r2 & 7) == (c2 >> 5)) & ((c2 & 31).astype(F32) == row_here))
    diagonal = rows((64, 64)) == cols((64, 64))
    bias_half = jnp.sum(jnp.where(diagonal, 0.5 * bias_ref[...], 0.0), axis=1, keepdims=True)
    bias_col[...] = jnp.broadcast_to(bias_half, (64, 256))

    spread = one_hot((cols((8, 256)) >> 5) == rows((8, 256)))
    for tap in range(9):
        lanes[tap] = 0.5 * dot(weight_ref[tap], spread, ((0,), (0,)))
    row_lanes = (cols((8, 256)) & 31).astype(F32)

    def fill(s):
        @pl.loop(8 * s, 8 * s + 8)
        def _(pair):
            start = pl.multiple_of(16 * pair, 16)
            delta = [row_lanes - row_col[pl.ds(start + 8 * k, 8)] for k in range(2)]
            for g in range(8):
                for dc in range(3):
                    parts = []
                    for k in range(2):
                        value = jnp.zeros((8, 256), F32)
                        for dr in range(3):
                            value = jnp.where(delta[k] == dr - 1.0, lanes[3 * dr + dc, 8 * g : 8 * g + 8], value)
                        parts.append(value)
                    both = jnp.concatenate(parts, axis=0).astype(BF16)
                    slot_band[g, pl.ds(start, 16), dc * 256 : (dc + 1) * 256] = both

    fill(0)
    for copy in edge_copies:
        copy.wait()
    from_left = jnp.where(tile > 0, edge_in[0], nought[:32, :128])
    from_right = jnp.where(tile < 7, edge_in[1], nought[:32, :128])

    def fix(g, f):
        n = 2 * g + f
        for i in range(8):
            span = slice(32 * i, 32 * i + 32)
            edge = pltpu.roll(from_left, (128 - 16 * i - n) % 128, 1)
            wide[n, span, 0:128] = jnp.where(lane == 0, edge, wide[n, span, 0:128])
            span = slice(512 + 32 * i, 544 + 32 * i)
            edge = pltpu.roll(from_right, 127 - 16 * i - n, 1)
            wide[n, span, 128:256] = jnp.where(lane == 127, edge, wide[n, span, 128:256])
        return f


    def slots(s, frames=(0, 1)):
        lo = 128 * s

        @pl.loop(0, 4, unroll=4)
        def _(pair):
            second = half_col[lo : lo + 128] > 0.5
            for f in frames:
                parts = []
                for e in range(2):
                    g = 2 * pair + e
                    act = dot(slot_band[g, lo : lo + 128, :], wide[2 * g + f])
                    plain = dot(pick[lo : lo + 128, :], wide[2 * g + f, 256:512])
                    act = jnp.where(second, act[:, 128:], act[:, :128]).reshape(16, 8, 128)
                    plain = jnp.where(second, plain[:, 128:], plain[:, :128]).reshape(16, 8, 128)
                    act = act + bias_col[pl.ds(8 * g, 8), 0:128]
                    parts.append(plain + gated(act))
                joined = jnp.concatenate(parts, axis=1).astype(BF16)
                outgoing[16 * s : 16 * s + 16, f, pl.ds(16 * pair, 16), :] = joined

    copies = []

    def send(stage, source, target, hops=HOPS):
        for hop in hops:
            to = peer(hop)
            copy = pltpu.make_async_remote_copy(
                src_ref=source(to),
                dst_ref=target,
                send_sem=send_sems.at[stage],
                recv_sem=recv_sems.at[stage],
                device_id={"frame": to},
                device_id_type=MESH,
            )
            copy.start()

    def whole(stage, ref):
        return pltpu.make_async_remote_copy(
            src_ref=ref,
            dst_ref=ref,
            send_sem=send_sems.at[stage],
            recv_sem=recv_sems.at[stage],
            device_id={"frame": peer(HOPS[0])},
            device_id_type=MESH,
        )

    for s in range(2):
        if s == 1:
            fill(1)
        if s == 0:
            for f in range(2):
                lax.fori_loop(0, 8, fix, f, unroll=8)
                slots(0, (f,))
                if f == 0:
                    pl.semaphore_wait(row_sem, 3)
                send(0, lambda to, f=f: outgoing.at[to, f], incoming.at[0, me, f], HOPS[:: 2 * f - 1])
        else:
            slots(1)
            whole(0, outgoing.at[pl.ds(0, 15)]).wait_send()
            send(1, lambda to: outgoing.at[16 + to], incoming.at[1, me])
        incoming[s, me] = outgoing[16 * s + me]

    offset = (cols((32, 256)) & 31) - rows((32, 256))

    @pl.loop(0, 8)
    def _(g):
        for dc in range(3):
            for o in range(8):
                value = jnp.zeros((32, 256), F32)
                for dr in range(3):
                    line = lanes[3 * dr + dc, pl.ds(8 * g + o, 1), :]
                    value = jnp.where(offset == dr - 1, line, value)
                band[g, o * 32 : (o + 1) * 32, dc * 256 : (dc + 1) * 256] = value.astype(BF16)

    expand = one_hot((cols((32, 256)) >> 3) == rows((32, 256)))
    row_lane = dot(jnp.broadcast_to(row_of, (8, 32)).astype(BF16), expand)[0:1]
    half_lane = dot(jnp.broadcast_to(half_of, (8, 32)).astype(BF16), expand)[0:1]
    live = (c2 >> 3) < count_ref[0]
    target = ((r2 >> 5) == (c2 & 7)) & ((r2 & 31).astype(F32) == row_lane) & live
    for h in range(2):
        chosen = jnp.where(target & (half_lane == float(h)), 1.0, 0.0)
        place[h * 256 : (h + 1) * 256, :] = chosen.astype(BF16)
        for s in range(2):
            found = jnp.sum(chosen[:, 128 * s : 128 * s + 128], axis=1, keepdims=True)
            cover = covered if s == 0 else covered_last
            cover[:, h * 128 : (h + 1) * 128] = jnp.broadcast_to(found, (256, 128)).astype(BF16)

    for layer in range(4):
        for j in range(3):
            line = 0.5 * depth_ref[j, layer : layer + 1, :]
            column = jnp.sum(jnp.where(diagonal, line, 0.0), axis=1, keepdims=True)
            taps[3 * layer + j] = jnp.broadcast_to(column, (64, 128))
    repeat = one_hot((rows((256, 64)) & 63) == cols((256, 64)))
    for layer in range(4):
        tall = dot(repeat, point_ref[layer]).astype(BF16)
        full = dot(tall, repeat, ((1,), (1,)))
        mix[layer] = jnp.where((r2 >> 6) == (c2 >> 6), full, 0.0).astype(BF16)

    @pl.loop(0, 8, unroll=2)
    def _(g):
        for f in range(2):
            act = dot(band[g], wide[2 * g + f])
            for o in range(8):
                half = act[o * 32 : (o + 1) * 32] + bias_col[pl.ds(8 * g + o, 1), :]
                value = cells[8 * g + o, f].astype(F32) + gated(half)
                out_ref[8 * g + o, f] = value.astype(BF16)

    def temporal(s):
        state[0:16] = jnp.zeros((16, 64, 128), F32)

        @pl.loop(0, 16, unroll=4)
        def _(p):
            state[pl.ds(16 + 2 * p, 2)] = incoming[s, p].astype(F32)

        for layer in range(4):
            d = 2**layer

            @pl.loop(0, 4, unroll=4)
            def _(i):
                base = 40 - 8 * i
                now = state[pl.ds(base, 8)]
                half = taps[3 * layer] * now
                half = half + taps[3 * layer + 1] * state[pl.ds(base - d, 8)]
                half = half + taps[3 * layer + 2] * state[pl.ds(base - 2 * d, 8)]
                squashed = gated(half).astype(BF16)
                pair = [squashed[0:4].reshape(256, 128), squashed[4:8].reshape(256, 128)]
                mixed = dot(mix[layer], jnp.concatenate(pair, axis=1))
                for h in range(2):
                    new = now[4 * h : 4 * h + 4] + mixed[:, 128 * h : 128 * h + 128].reshape(4, 64, 128)
                    if layer < 3:
                        state[pl.ds(base + 4 * h, 4)] = new
                    else:
                        answer[s, pl.ds(12 - 4 * i + 2 * h, 2)] = new.reshape(2, 2, 64, 128).astype(BF16)

    for s in range(2):
        whole(s, incoming.at[s, pl.ds(0, 15)]).wait_recv()
        temporal(s)
        send(2 + s, lambda to, s=s: answer.at[s, to], returned.at[16 * s + me])
        returned[16 * s + me] = answer[s, me]

    for s in range(2):
        whole(2 + s, returned.at[pl.ds(0, 15)]).wait_recv()
        if s == 0:
            pl.loop(0, 4, unroll=2)(functools.partial(merge, s, out_ref, out_ref, returned, place, covered))

    for s in range(2):
        if s:
            whole(s, outgoing.at[pl.ds(0, 15)]).wait_send()
        whole(2 + s, answer.at[s, pl.ds(0, 15)]).wait_send()


def merge(s, old_ref, new_ref, returned, place, covered, pair):
    split = [returned[16 * s : 16 * s + 16, f, pl.ds(16 * pair, 16), :].astype(F32) for f in range(2)]
    for e in range(2):
        g = 2 * pair + e
        both = [part[:, 8 * e : 8 * e + 8].reshape(128, 128) for part in split]
        value = dot(place[:, 128 * s : 128 * s + 128], jnp.concatenate(both, axis=1).astype(BF16))
        for f in range(2):
            for h in range(2):
                span = slice(128 * h, 128 * h + 128)
                new = value[256 * h : 256 * h + 256, 128 * f : 128 * f + 128]
                old = old_ref[pl.ds(8 * g, 8), f, :, span].reshape(256, 128)
                new = jnp.where(covered[:, span] > 0, new.astype(BF16), old)
                new_ref[pl.ds(8 * g, 8), f, :, span] = new.reshape(8, 32, 128)


def finish(old_ref, returned, place, covered, out_hbm, out, sems):
    copies = []
    for pair in range(4):
        merge(1, old_ref, out, returned, place, covered, pair)
        span = pl.ds(16 * pair, 16)
        copies.append(pltpu.make_async_copy(out.at[span], out_hbm.at[span], sems.at[pair]))
        copies[pair].start()
    for copy in copies:
        copy.wait()


def on_device(grid, conv_weight, conv_bias, depth_kernel, point_weight, occupied, counts):
    buffers = [
        ((64, 2, 32, 256), BF16),
        ((16, 768, 256), BF16),
        ((9, 64, 256), F32),
        ((8, 256, 768), BF16),
        ((8, 256, 768), BF16),
        ((256, 256), BF16),
        ((256, 256), BF16),
        ((4, 256, 256), BF16),
        ((12, 64, 128), F32),
        ((64, 256), F32),
        ((256, 256), F32),
        ((256, 128), F32),
        ((2, 32, 128), BF16),
        ((2, 32, 128), BF16),
        ((32, 2, 64, 128), BF16),
        ((2, 16, 2, 64, 128), BF16),
        ((48, 64, 128), F32),
        ((2, 16, 2, 64, 128), BF16),
    ]
    kinds = [(grid.shape, BF16), ((32, 2, 64, 128), BF16), ((512, 256), BF16), ((256, 256), BF16)]
    vmem = pl.BlockSpec(memory_space=pltpu.VMEM)
    parts = pl.pallas_call(
        kernel,
        out_shape=[jax.ShapeDtypeStruct(shape, kind) for shape, kind in kinds],
        in_specs=[pl.BlockSpec(memory_space=pltpu.HBM)] * 7,
        out_specs=[vmem] * 4,
        scratch_shapes=[
            pltpu.VMEM((9, 8, 64), BF16),
            pltpu.VMEM((1, 64), F32),
            pltpu.VMEM((3, 4, 64), F32),
            pltpu.VMEM((4, 64, 64), BF16),
            pltpu.VMEM((1, 32), jnp.int32),
            pltpu.SMEM((1,), jnp.int32),
        ]
        + [pltpu.VMEM(shape, kind) for shape, kind in buffers]
        + [
            pltpu.SemaphoreType.DMA((11,)),
            pltpu.SemaphoreType.DMA((2,)),
            pltpu.SemaphoreType.DMA((2,)),
            pltpu.SemaphoreType.DMA((4,)),
            pltpu.SemaphoreType.DMA((4,)),
            pltpu.SemaphoreType.REGULAR,
        ],
        compiler_params=pltpu.CompilerParams(
            collective_id=0, has_side_effects=True, vmem_limit_bytes=36 * 1024 * 1024
        ),
        cost_estimate=pl.CostEstimate(flops=4_000_000_000, bytes_accessed=0, transcendentals=3 << 20),
    )(
        *(
            pltpu.with_memory_space_constraint(array, pltpu.HBM)
            for array in (
                grid,
                conv_weight.transpose(0, 2, 1),
                conv_bias.reshape(1, 64),
                depth_kernel.transpose(1, 0, 2),
                point_weight,
                occupied,
            )
        ),
        counts,
    )
    return pl.pallas_call(
        finish,
        out_shape=jax.ShapeDtypeStruct(grid.shape, grid.dtype),
        in_specs=[vmem] * 4,
        out_specs=pl.BlockSpec(memory_space=pl.ANY),
        scratch_shapes=[pltpu.VMEM(grid.shape, BF16), pltpu.SemaphoreType.DMA((4,))],
        compiler_params=pltpu.CompilerParams(vmem_limit_bytes=36 * 1024 * 1024),
    )(*parts)


def solution(mesh):
    placed = (P(None, "frame", None, "tile"), P(), P(), P(), P(), P("tile", None), P("tile"))
    return jax.shard_map(
        on_device,
        mesh=mesh,
        in_specs=placed,
        out_specs=P(None, "frame", None, "tile"),
        check_vma=False,
    )
```
